32 devices in a mesh: grp: 2 (over y), dim: 4 (over z), ex: 4 (over x, core).
Axes of the slice: x: 2, y: 2, z: 4, core: 2. Of those that a mesh axis runs over, the one named last changes fastest.
Arguments:
- store: bfloat16 [2048, 32768], P(('grp', 'ex'), 'dim'), parts along dimension 0, may hold values from -1000 to 1000
- queries: bfloat16 [256, 32768], P(('grp', 'ex'), 'dim'), parts along dimension 0, may hold values from -24 to 24
- eig_left: float32 [16, 64, 64], P(('grp', 'dim')), parts along dimension 0, may hold values from -1 to 1
- eig_right: float32 [16, 64, 64], P(('grp', 'dim')), parts along dimension 0, may hold values from -1 to 1
- val_left: float32 [16, 64], P(('grp', 'dim')), parts along dimension 0, may hold values from 0.01 to 10
- val_right: float32 [16, 64], P(('grp', 'dim')), parts along dimension 0, may hold values from 0.01 to 10
Outputs:
- scores: float32 [2048, 128], P(('grp', 'ex'), 'dim'), parts along dimension 0
The draws below stay inside these ranges and needn't reach their ends.
There are 2 independent parts, one for each index of `grp`. The reference program is written for one: setup_inputs(seed, part) draws one part's arguments, and reference() takes and returns one part's arrays. A program takes and returns all parts, laid end to end along the dimension named above; each array names one. Nothing has to cross between parts.
All inputs are finite; a program needn't handle non-finite values.
Results may differ from the reference program's by a relative error of at most 0.0029.
Values may be sent and summed in bfloat16 or wider, within the bound.
No kernel may reach another device: no remote copies, remote signals or barrier semaphores. Data moves between devices by JAX's collectives and lax.ppermute only.
A program may use at most 64 MiB of HBM per device.

```python
import jax
import jax.numpy as jnp
from jax import lax

PA = 64
PB = 64
LAYERS = 8
P_SIZE = 32768
NTRAIN = 1024
NQ = 128


def cosine_table(count):
    rows = jnp.arange(count, dtype=jnp.float32)[:, None]
    freqs = jnp.arange(count, dtype=jnp.float32)[None, :]
    table = jnp.sqrt(2.0 / count) * jnp.cos(jnp.pi * (rows + 0.5) * freqs / count)
    return jnp.where(freqs == 0.0, jnp.sqrt(1.0 / count), table)


def eigen_basis(key, count):
    key_perm, key_sign = jax.random.split(key)
    orders = jax.vmap(lambda item: jax.random.permutation(item, count))(jax.random.split(key_perm, LAYERS))
    signs = (2 * jax.random.randint(key_sign, (LAYERS, count), 0, 2) - 1).astype(jnp.float32)
    table = cosine_table(count)
    picked = jnp.transpose(table[:, orders], (1, 0, 2))
    return picked * signs[:, None, :]


def factors(key):
    key = jax.random.fold_in(key, 500)
    key_a, key_b, key_c, key_d = jax.random.split(key, 4)
    basis_left = eigen_basis(key_a, PA)
    basis_right = eigen_basis(key_b, PB)
    low = jnp.log(0.01)
    high = jnp.log(10.0)
    values_left = jnp.exp(jax.random.uniform(key_c, (LAYERS, PA), jnp.float32, low, high))
    values_right = jnp.exp(jax.random.uniform(key_d, (LAYERS, PB), jnp.float32, low, high))
    return (basis_left, basis_right, values_left, values_right)


def draw_eig_left(key, part):
    return factors(key)[0]


def draw_eig_right(key, part):
    return factors(key)[1]


def draw_val_left(key, part):
    return factors(key)[2]


def draw_val_right(key, part):
    return factors(key)[3]


def draw_store(key, part):
    basis_left, basis_right, values_left, values_right = factors(key)
    key = jax.random.fold_in(key, 11)
    key_z, key_row, key_layer = jax.random.split(key, 3)
    rise = 3.0 ** (jnp.arange(LAYERS, dtype=jnp.float32) / max(LAYERS - 1, 1))
    jitter = jnp.exp(jax.random.uniform(key_layer, (LAYERS,), jnp.float32, 0.0, jnp.log(2.0)))
    layer_scale = rise * jitter
    row_scale = jnp.exp(jax.random.uniform(key_row, (NTRAIN,), jnp.float32, 0.0, jnp.log(10.0)))

    def one_layer(index):
        key_here = jax.random.fold_in(key_z, index)
        values = jnp.clip(jax.random.normal(key_here, (NTRAIN, PA, PB), jnp.float32), -6.0, 6.0)
        coeff = values * (0.3 * layer_scale[index])
        block = jnp.einsum('ai,nij,bj->nab', basis_left[index], coeff, basis_right[index], precision=lax.Precision.HIGHEST)
        block = block * row_scale[:, None, None]
        return jnp.clip(block, -1000.0, 1000.0).astype(jnp.bfloat16).reshape(NTRAIN, PA * PB)
    blocks = lax.map(one_layer, jnp.arange(LAYERS))
    return jnp.transpose(blocks, (1, 0, 2)).reshape(NTRAIN, P_SIZE)


def levels(rng, shape, cuts, least, largest):
    loudness, own = 1.0, jax.random.fold_in(rng, 6)
    for position, parts in cuts:
        heights = jnp.exp(jax.random.uniform(jax.random.fold_in(own, position), (parts,), jnp.float32, least / len(cuts), largest / len(cuts)))
        loudness = loudness * jnp.repeat(heights, shape[position] // parts).reshape([-1 if axis == position else 1 for axis in range(len(shape))])
    return loudness


def scatter_about(own_key, shape, spread, most, pieces=(), kind=jnp.bfloat16):
    loudness = levels(own_key, shape, pieces, -0.22, 0.18) if pieces else 1.0
    entries = jax.random.normal(own_key, shape, jnp.float32) * spread * loudness
    return jnp.minimum(jnp.maximum(entries, -most), most).astype(kind)


def setup_inputs(seed: int = 0, part: int = 0) -> dict:
    key_list = jax.random.split(jax.random.key(seed), 7)
    own_keys = jax.random.split(jax.random.fold_in(key_list[6], part), 7)
    store = draw_store(jax.random.fold_in(jax.random.fold_in(key_list[6], part), 71), part)
    queries = scatter_about(own_keys[1], (NQ, P_SIZE), 4.0, 24.0, ((0, 4), (1, 4)))
    eig_left = draw_eig_left(jax.random.fold_in(jax.random.fold_in(key_list[6], part), 71), part)
    eig_right = draw_eig_right(jax.random.fold_in(jax.random.fold_in(key_list[6], part), 71), part)
    val_left = draw_val_left(jax.random.fold_in(jax.random.fold_in(key_list[6], part), 71), part)
    val_right = draw_val_right(jax.random.fold_in(jax.random.fold_in(key_list[6], part), 71), part)
    return {"store": store, "queries": queries, "eig_left": eig_left, "eig_right": eig_right, "val_left": val_left, "val_right": val_right}


damping = 0.1

def precondition(queries, eig_left, eig_right, val_left, val_right):
    count = queries.shape[0]
    layers = eig_left.shape[0]
    side_a = eig_left.shape[1]
    side_b = eig_right.shape[1]
    block = queries.astype(jnp.float32).reshape(count, layers, side_a, side_b)
    high = lax.Precision.HIGHEST
    rotated = jnp.einsum('lai,nlab->nlib', eig_left, block, precision=high)
    rotated = jnp.einsum('nlib,lbj->nlij', rotated, eig_right, precision=high)
    scaled = rotated / (val_left[None, :, :, None] * val_right[None, :, None, :] + damping)
    back = jnp.einsum('lai,nlij->nlaj', eig_left, scaled, precision=high)
    back = jnp.einsum('nlaj,lbj->nlab', back, eig_right, precision=high)
    return back.reshape(count, layers * side_a * side_b).astype(jnp.bfloat16)

def reference(store, queries, eig_left, eig_right, val_left, val_right):
    precond = precondition(queries, eig_left, eig_right, val_left, val_right)
    raw = lax.dot_general(store, precond, (((1,), (1,)), ((), ())), preferred_element_type=jnp.float32)
    squares = lax.optimization_barrier(jnp.sum(jnp.square(store.astype(jnp.float32)), axis=1))
    norm = jnp.sqrt(squares + 1e-06)
    return raw / norm[:, None]
```

```python
import functools

import jax
import jax.numpy as jnp
from jax import lax
from jax.experimental import pallas as pl
from jax.experimental.pallas import tpu as pltpu
from jax.sharding import PartitionSpec as P

damping = 0.1
f32, bf16 = jnp.float32, jnp.bfloat16
WHOLE = pl.BlockSpec(memory_space=pltpu.VMEM)
HBM = pl.BlockSpec(memory_space=pl.ANY)
SIDE = 64
LANES = 128
QUAD = 4
PAIRS = SIDE // 2
FLAT = SIDE * SIDE


def near(x):
    return pltpu.with_memory_space_constraint(x, pltpu.VMEM)


def call(body, name, outs, ins, scratch=(), flops=0, moved=0, specs=None):
    return pl.pallas_call(
        body,
        out_shape=outs,
        in_specs=specs or [WHOLE] * len(ins),
        out_specs=jax.tree.map(lambda _: WHOLE, outs, is_leaf=lambda o: hasattr(o, "shape")),
        scratch_shapes=scratch,
        cost_estimate=pl.CostEstimate(flops=flops, bytes_accessed=moved, transcendentals=0),
        compiler_params=pltpu.CompilerParams(vmem_limit_bytes=40 * 2**20),
        name=name,
    )(*ins)


def split(x):
    high = x.astype(bf16)
    return high, (x - high.astype(f32)).astype(bf16)


def mm(a, b):
    return jnp.dot(a, b, preferred_element_type=f32)


def factors_body(queries, left, right, val_left, val_right, *refs):
    to_high, to_low, back_high, back_low, turn, unturn, unturn_low, inverse = refs[:8]
    copies = []
    for layer, here in enumerate(refs[8:-1]):
        part = pl.ds(layer * FLAT, FLAT)
        copies.append(pltpu.make_async_copy(queries.at[:, part], here, refs[-1].at[layer]))
        copies[-1].start()
    for layer in range(left.shape[0]):
        block = lax.broadcasted_iota(jnp.int32, (PAIRS, QUAD * SIDE), 1) // SIDE
        rows = []
        for low in range(2):
            part = left[layer, pl.ds(low, PAIRS, stride=2), :]
            wide = jnp.concatenate([part] * QUAD, axis=1)
            rows += [jnp.where(block == quad, wide, 0.0) for quad in range(QUAD)]
        table = jnp.concatenate(rows, axis=0)
        to_high[layer], to_low[layer] = split(table)
        back_high[layer], back_low[layer] = split(table.T)
        twice = jnp.concatenate([right[layer]] * 2, axis=1)
        half = lax.broadcasted_iota(jnp.int32, (SIDE, LANES), 1) // SIDE
        table = jnp.concatenate([jnp.where(half == low, twice, 0.0) for low in range(2)], axis=0)
        turn[layer] = jnp.concatenate(split(table), axis=0)
        high, rest = split(table.T)
        unturn[layer] = jnp.concatenate([high, high], axis=0)
        unturn_low[layer] = rest
        along = jnp.concatenate([val_left[layer : layer + 1, :]] * QUAD, axis=1)
        down = jnp.broadcast_to(val_right[layer : layer + 1, :], (SIDE, SIDE)).T
        inverse[layer] = 1.0 / (along * jnp.concatenate([down] * QUAD, axis=1) + damping)
    for copy in copies:
        copy.wait()


def factors(queries, left, right, val_left, val_right):
    layers = left.shape[0]
    shapes = [((256, 256), bf16)] * 4 + [((256, 128), bf16)] * 2 + [((128, 128), bf16), ((64, 256), f32)]
    outs = [pltpu.VMEM((layers, *shape), kind) for shape, kind in shapes]
    outs += [pltpu.VMEM((queries.shape[0], FLAT), bf16)] * layers
    outs = call(
        factors_body,
        "factors",
        outs,
        (queries, left, right, val_left, val_right),
        [pltpu.SemaphoreType.DMA((layers,))],
        flops=10**6,
        moved=2**20,
        specs=[HBM] + [WHOLE] * 4,
    )
    return outs[:8], outs[8:]


def precondition_body(layer, queries, *refs):
    tables, outs, buffer = refs[:8], refs[8:-1], refs[-1]
    to_high, to_low, back_high, back_low, turn, unturn, unturn_low, inverse = [r[layer] for r in tables]
    count = queries.shape[0]
    groups = count // QUAD
    x = jnp.concatenate([queries[:, a * LANES : (a + 1) * LANES] for a in range(PAIRS)], axis=0)
    buffer[...] = mm(jnp.concatenate([x, x], axis=1), turn)
    turned = []
    for group in range(groups):
        t = jnp.concatenate([buffer[pl.ds(QUAD * group + k, PAIRS, stride=count), :] for k in range(QUAD)], axis=0).T
        turned.append(jnp.concatenate([t[:SIDE], t[SIDE:]], axis=1))
    high, low = split(jnp.concatenate(turned, axis=0))
    t = mm(high, to_high) + (mm(low, to_high) + mm(high, to_low))
    high, low = split(t * jnp.concatenate([inverse] * groups, axis=0))
    t = mm(high, back_high) + (mm(low, back_high) + mm(high, back_low))
    rows = []
    for group in range(groups):
        u = t[SIDE * group : SIDE * (group + 1)]
        rows.append(jnp.concatenate([u[:, :LANES], u[:, LANES:]], axis=0).T)
    high, low = split(jnp.concatenate(rows, axis=0))
    buffer[...] = mm(jnp.concatenate([high, low], axis=1), unturn) + mm(high, unturn_low)
    a = 0
    for out in outs:
        for column in range(0, out.shape[1], LANES):
            out[:, column : column + LANES] = buffer[pl.ds(a, count, stride=PAIRS), :].astype(bf16)
            a += 1


def precondition(queries, tables, layer, widths):
    count = queries.shape[0]
    outs = [pltpu.VMEM((count, width), bf16) for width in widths]
    return call(
        functools.partial(precondition_body, layer),
        f"precondition_{layer}",
        outs,
        [near(x) for x in (queries, *tables)],
        [pltpu.VMEM((count * PAIRS, LANES), f32)],
        flops=count * FLAT * SIDE * 8 * 3,
        moved=2 * 2**20,
    )


def squares_body(store, held, out, sems):
    rows, columns = store.shape
    width = min(columns, 1024)
    copies = []
    for index in range(columns // width):
        part = pl.ds(index * width, width)
        copies.append(pltpu.make_async_copy(store.at[:, part], held.at[:, part], sems.at[index]))
        copies[-1].start()
    total = jnp.zeros((rows, LANES), f32)
    for index, copy in enumerate(copies):
        copy.wait()
        for column in range(index * width, (index + 1) * width, LANES):
            x = held[:, column : column + LANES].astype(f32)
            total += x * x
    out[...] = jnp.broadcast_to(jnp.sum(total.T, axis=0, keepdims=True), out.shape)


def squares(store):
    rows, columns = store.shape
    return call(
        squares_body,
        "squares",
        [pltpu.VMEM((rows, columns), bf16), pltpu.VMEM((8, rows), f32)],
        (store,),
        [pltpu.SemaphoreType.DMA((max(1, columns // 1024),))],
        flops=2 * rows * columns,
        moved=8 * 2**20,
        specs=[HBM],
    )


def dot_rows(pieces, held, first):
    x = jnp.concatenate([p[...] for p in pieces], axis=0)
    return lax.dot_general(x, held[:, first : first + x.shape[1]], (((1,), (1,)), ((), ())), preferred_element_type=f32)


def partial_body(first, started, *refs):
    held, pieces, out = refs[0], refs[1 + started : -1], refs[-1]
    value = dot_rows(pieces, held, first)
    out[...] = refs[1][...] + value if started else value


def last_body(first, partners, *refs):
    held, before, sq, pieces = refs[0], refs[1], refs[2], refs[3 : -len(partners) - 1]
    outs, total = refs[-len(partners) - 1 : -1], refs[-1]
    total[...] = before[...] + dot_rows(pieces, held, first)
    count = pieces[0].shape[0]
    ex, dim = lax.axis_index("ex"), lax.axis_index("dim")
    chips = len(pieces) // 2
    for out, partner in zip(outs, partners):
        block = partner(dim)
        apart = lax.rem(ex // 2 - block // 2 + chips, chips)
        place = 2 * apart + (ex % 2 + block % 2) % 2
        out[:count] = total[pl.ds(pl.multiple_of(place * count, count), count), :]
        out[count:] = sq[...]


def finish_body(*refs):
    out = refs[-1]
    total = refs[0][...]
    for r in refs[1:-1]:
        total = total + r[...]
    count = out.shape[1]
    scores = total[:count] / jnp.sqrt(total[count : count + 1] + 1e-06)
    out[...] = scores.T


def local(dims, exs, store, queries, eig_left, eig_right, val_left, val_right):
    layers = eig_left.shape[0]
    count, rows = queries.shape[0], store.shape[0]
    chips = exs // 2
    across = [(e, e ^ 1) for e in range(exs)]

    tables, here = factors(queries, eig_left, eig_right, val_left, val_right)
    pieces = []
    for layer in range(layers):
        widths = (FLAT,) if layer < layers - 1 else (FLAT // 2, FLAT // 2)
        pieces += precondition(here[layer], tables, layer, widths)
    held, sq = squares(store)

    total, first = None, 0
    for index, piece in enumerate(pieces):
        parts = [piece, lax.ppermute(piece, "ex", across)]
        for step in range(1, chips):
            came = lax.ppermute(piece, "ex", [(e, (e + 2 * step) % exs) for e in range(exs)])
            parts += [came, lax.ppermute(came, "ex", across)]
        width = piece.shape[1]
        ins = (held, *(() if total is None else (total,)), *((sq,) if index == len(pieces) - 1 else ()), *parts)
        ins = [near(x) for x in ins]
        cost = dict(flops=2 * count * exs * rows * width, moved=2 * 2**20)
        if index < len(pieces) - 1:
            body = functools.partial(partial_body, first, int(index > 0))
            total = call(body, f"scores_{index}", pltpu.VMEM((count * exs, rows), f32), ins, **cost)
        else:
            if dims & (dims - 1):
                links = [[(z, (z + k) % dims) for z in range(dims)] for k in range(dims)]
                partners = [lambda z, k=k: lax.rem(z + k, dims) for k in range(dims)]
            else:
                links = [[(z, z ^ k) for z in range(dims)] for k in range(dims)]
                partners = [lambda z, k=k: lax.bitwise_xor(z, k) for k in range(dims)]
            body = functools.partial(last_body, first, partners)
            outs = [pltpu.VMEM((count + 8, rows), f32) for _ in range(dims)]
            sent = call(body, "scores_last", outs, ins, [pltpu.VMEM((count * exs, rows), f32)], **cost)
        first += width
    came = [sent[0]] + [lax.ppermute(sent[k], "dim", links[k]) for k in reversed(range(1, dims))]
    return call(
        finish_body, "finish", jax.ShapeDtypeStruct((rows, count), f32), [near(c) for c in came], flops=10**6, moved=2**20
    )


def solution(mesh):
    in_specs = (
        P(("grp", "ex"), "dim"),
        P(("grp", "ex"), "dim"),
        P(("grp", "dim"), None, None),
        P(("grp", "dim"), None, None),
        P(("grp", "dim"), None),
        P(("grp", "dim"), None),
    )
    out_specs = P(("grp", "ex"), "dim")
    body = functools.partial(local, mesh.shape["dim"], mesh.shape["ex"])
    return jax.shard_map(body, mesh=mesh, in_specs=in_specs, out_specs=out_specs, check_vma=False)
```

```python
import functools

import jax
import jax.numpy as jnp
from jax import lax
from jax.experimental import pallas as pl
from jax.experimental.pallas import tpu as pltpu
from jax.sharding import PartitionSpec as P

damping = 0.1
f32, bf16 = jnp.float32, jnp.bfloat16
WHOLE = pl.BlockSpec(memory_space=pltpu.VMEM)
HBM = pl.BlockSpec(memory_space=pltpu.HBM)
SIDE = 64
SCALE = 0.02
LANES = 128
QUAD = 4
PAIRS = SIDE // 2
FLAT = SIDE * SIDE
PAD = 8
ROWS = 16


def near(x):
    return pltpu.with_memory_space_constraint(x, pltpu.VMEM)


def far(x):
    return pltpu.with_memory_space_constraint(x, pltpu.HBM)


def after(x, *others):
    return lax.optimization_barrier((x, *others))[0]


def call(body, name, outs, ins, scratch=(), us=1.0, specs=None, to=WHOLE):
    return pl.pallas_call(
        body,
        out_shape=outs,
        in_specs=specs or [WHOLE] * len(ins),
        out_specs=jax.tree.map(lambda _: to, outs, is_leaf=lambda o: hasattr(o, "shape")),
        scratch_shapes=scratch,
        cost_estimate=pl.CostEstimate(flops=int(us * 1.15e9 * SCALE), bytes_accessed=0, transcendentals=0),
        compiler_params=pltpu.CompilerParams(vmem_limit_bytes=40 * 2**20),
        name=name,
    )(*ins)


def split(x):
    high = x.astype(bf16)
    return high, (x - high.astype(f32)).astype(bf16)


def mm(a, b):
    return jnp.dot(a, b, preferred_element_type=f32)


def position():
    ex, dim = lax.axis_index("ex"), lax.axis_index("dim")
    return ex // 2, ex % 2, dim


def three(x):
    high, low = split(x)
    return jnp.concatenate([high, low, high], axis=1)


def stacked(table):
    high, low = split(table)
    return jnp.concatenate([high, high, low], axis=0)


def factors_body(*refs):
    given, (left, right, val_left, val_right), sems = refs[:5], refs[-5:-1], refs[-1]
    forth, back, turn, unturn, inverse, own = refs[5:11]
    layer = position()[1]
    copies = []
    for k, (g, h) in enumerate(zip(given, [left, right, val_left, val_right, own])):
        copies.append(pltpu.make_async_copy(g.at[layer] if k < 2 else g, h, sems.at[k]))
        copies[-1].start()
    for copy in copies[:4]:
        copy.wait()
    block = lax.broadcasted_iota(jnp.int32, (PAIRS, QUAD * SIDE), 1) // SIDE
    rows = []
    for low in range(2):
        part = left[pl.ds(low, PAIRS, stride=2), :]
        wide = jnp.concatenate([part] * QUAD, axis=1)
        rows += [jnp.where(block == quad, wide, 0.0) for quad in range(QUAD)]
    table = jnp.concatenate(rows, axis=0)
    forth[...] = stacked(table)
    back[...] = stacked(table.T)
    twice = jnp.concatenate([right[...]] * 2, axis=1)
    half = lax.broadcasted_iota(jnp.int32, (SIDE, LANES), 1) // SIDE
    table = jnp.concatenate([jnp.where(half == low, twice, 0.0) for low in range(2)], axis=0)
    turn[...] = jnp.concatenate(split(table), axis=0)
    unturn[...] = stacked(table.T)
    along = jnp.concatenate([val_left[pl.ds(layer, 1), :]] * QUAD, axis=1)
    down = jnp.broadcast_to(val_right[pl.ds(layer, 1), :], (SIDE, SIDE)).T
    inverse[...] = 1.0 / (along * jnp.concatenate([down] * QUAD, axis=1) + damping)
    copies[4].wait()


def factors(queries, left, right, val_left, val_right):
    shapes = [((768, 256), bf16)] * 2 + [((256, 128), bf16), ((384, 128), bf16), ((64, 256), f32), (queries.shape, bf16)]
    given = (left, right, val_left, val_right, queries)
    *tables, own = call(
        factors_body,
        "factors",
        [pltpu.VMEM(shape, kind) for shape, kind in shapes],
        [far(x) for x in given],
        [pltpu.VMEM(x.shape[1:] if x.ndim == 3 else x.shape, f32) for x in given[:4]] + [pltpu.SemaphoreType.DMA((5,))],
        us=1.2,
        specs=[HBM] * 5,
    )
    return tables, own


def precondition_body(parity, first, joined, own, other, *refs):
    forth, back, turn, unturn, inverse = refs[:5]
    outs, buffer = refs[5:-1], refs[-1]
    outs, union = (outs[:-1], outs[-1]) if joined else (outs, None)
    _, core, dim = position()
    count = outs[0].shape[0]
    groups = count // QUAD
    pitch, pitch_back = count + PAD, PAIRS + PAD
    mine = (core + dim) % 2 == parity
    x = []
    for a in range(PAIRS):
        part = pl.ds(pl.multiple_of(core * FLAT + a * LANES, LANES), LANES)
        x.append(jnp.where(mine, own[first : first + count, part], other[first : first + count, part]))
    x = jnp.concatenate(x, axis=0)
    t = mm(jnp.concatenate([x, x], axis=1), turn[...])
    for a in range(PAIRS):
        buffer[a * pitch : a * pitch + count] = t[a * count : (a + 1) * count]
    turned = []
    for group in range(groups):
        t = jnp.concatenate([buffer[pl.ds(QUAD * group + k, PAIRS, stride=pitch), :] for k in range(QUAD)], axis=0).T
        turned.append(jnp.concatenate([t[:SIDE], t[SIDE:]], axis=1))
    t = mm(three(jnp.concatenate(turned, axis=0)), forth[...])
    t = mm(three(t * jnp.concatenate([inverse[...]] * groups, axis=0)), back[...])
    rows = []
    for group in range(groups):
        u = t[SIDE * group : SIDE * (group + 1)]
        rows.append(jnp.concatenate([u[:, :LANES], u[:, LANES:]], axis=0).T)
    t = mm(three(jnp.concatenate(rows, axis=0)), unturn[...])
    for n in range(count):
        buffer[n * pitch_back : n * pitch_back + PAIRS] = t[n * PAIRS : (n + 1) * PAIRS]
    a = 0
    for out in outs:
        for column in range(0, out.shape[1], LANES):
            part = buffer[pl.ds(a, count, stride=pitch_back), :].astype(bf16)
            out[:, column : column + LANES] = part
            if joined:
                union[:, a * LANES : (a + 1) * LANES] = part
            a += 1


def precondition(own, other, tables, parity, first, count, widths, joined=False):
    widths = widths + [FLAT] * joined
    return call(
        functools.partial(precondition_body, parity, first, joined),
        f"precondition_{parity}_{first}",
        [pltpu.VMEM((count, width), bf16) for width in widths],
        [near(x) for x in (own, other, *tables)],
        [pltpu.VMEM((max(PAIRS * (count + PAD), count * (PAIRS + PAD)), LANES), f32)],
        us=1.8 * count / 32,
    )


def dot_cores(core, ours, theirs, store, first):
    value = 0.0
    for layer, x in ((core, ours), (1 - core, theirs)):
        value = value + mm(x, store[pl.ds(pl.multiple_of(layer * FLAT + first, LANES), x.shape[1]), :])
    return value


def store_body(store, turned, out):
    rows, columns = store.shape
    squares = jnp.zeros((8, rows), f32)
    for column in range(0, columns, rows):
        part = store[:, column : column + rows].T
        turned[column : column + rows] = part
        part = part.astype(f32)
        squares += jnp.sum((part * part).reshape(-1, 8, rows), axis=0)
    out[...] = jnp.broadcast_to(jnp.sum(squares, axis=0, keepdims=True), out.shape)


def gathered(core, widths, first, refs, chips, store):
    ours, theirs, pairs = refs[0], refs[1], refs[2:]
    value, away = 0.0, chips - 1
    for index, width in enumerate(widths):
        sides = []
        for k, mine in enumerate((ours, theirs)):
            came = pairs[2 * away * index + away * k : 2 * away * index + away * (k + 1)]
            sides.append(jnp.concatenate([mine[:, first : first + width], *[r[...] for r in came]], axis=0))
        value = value + dot_cores(core, *sides, store, first)
        first += width
    return value


def odd_body(chips, store, sq, *refs):
    pieces, (message, total) = refs[:-2], refs[-2:]
    x, core, _ = position()
    half = len(pieces) // 2
    sides = [jnp.concatenate([r[...] for r in pieces[k * half : (k + 1) * half]], axis=0) for k in range(2)]
    total[...] = dot_cores(core, *sides, store, 0)
    count = total.shape[0] // chips
    for block in range(chips):
        apart = lax.rem(x - block + chips, chips)
        message[block * count : (block + 1) * count] = total[pl.ds(pl.multiple_of(apart * count, count), count), :]
    message[chips * count :] = sq[...]


def even_body(chips, widths, store, *refs):
    _, core, _ = position()
    refs[-1][...] = gathered(core, widths, 0, refs[:-1], chips, store)


def send_body(chips, widths, first, partners, store, sq, got, before, *refs):
    refs, messages, total = refs[: -1 - len(partners)], refs[-1 - len(partners) : -1], refs[-1]
    x, core, dim = position()
    total[...] = before[...] + gathered(core, widths, first, refs, chips, store)
    count = refs[0].shape[0]
    for message, partner in zip(messages, partners):
        block = partner(dim) // 2
        apart = lax.rem(x - block + chips, chips)
        message[:count] = (
            got[pl.ds(pl.multiple_of(block * count, count), count), :]
            + total[pl.ds(pl.multiple_of(apart * count, count), count), :]
        )
        message[count:] = sq[...] + got[chips * count :]


def finish_body(*refs):
    out, here, sem = refs[-3:]
    total = refs[0][...]
    for r in refs[1:-3]:
        total = total + r[...]
    count = out.shape[0]
    here[...] = total[:count] / jnp.sqrt(total[count : count + 1] + 1e-06)
    copy = pltpu.make_async_copy(here, out, sem)
    copy.start()
    copy.wait()


def local(dims, exs, store, queries, eig_left, eig_right, val_left, val_right):
    count, rows = queries.shape[0], store.shape[0]
    chips = exs // 2
    across = [(e, e ^ 1) for e in range(exs)]

    def swap(x):
        return lax.ppermute(x, "ex", across)

    def hop(x, step):
        return lax.ppermute(x, "ex", [(e, (e + 2 * step) % exs) for e in range(exs)])

    other = swap(queries)
    tables, own = factors(queries, eig_left, eig_right, val_left, val_right)
    odd, odd_came, theirs_odd = [], [], []
    for first in range(0, count, ROWS):
        given = after(own, *theirs_odd)
        odd += precondition(given, other, tables, 1, first, ROWS, [FLAT])
        odd_came.append([hop(odd[-1], step) for step in range(1, chips)])
        theirs_odd.append(swap(odd[-1]))
    widths = [FLAT * 5 // 8, FLAT * 3 // 8]
    *even, ours = precondition(after(own, odd[-1]), other, tables, 0, 0, count, widths, True)
    outs = [pltpu.VMEM((store.shape[1], rows), bf16), pltpu.VMEM((8, rows), f32)]
    store, sq = call(store_body, "store", outs, [near(after(store, *even))], us=1.5)
    even_came = [[hop(p, step) for step in range(1, chips)] for p in even]
    theirs = swap(ours)

    odd_came = [[after(x, *even, sq) for x in xs] for xs in odd_came]
    came = [x for step in zip(*odd_came) for x in step]
    ins = [store, sq, *odd, *came, *theirs_odd, *[swap(x) for x in came]]
    body = functools.partial(odd_body, chips)
    out = pltpu.VMEM((chips * count + 8, rows), f32)
    scratch = [pltpu.VMEM((count * chips, rows), f32)]
    message = call(body, "odd", out, [near(x) for x in ins], scratch, us=1.4)
    got = lax.ppermute(message, "dim", [(z, z ^ 1) for z in range(dims)])

    even_came = [[after(x, message) for x in xs] for xs in even_came]
    even_came[1] = [after(x, got) for x in even_came[1]]
    pairs = [[*xs, *[swap(x) for x in xs]] for xs in even_came]
    body = functools.partial(even_body, chips, widths[:1])
    ins = [store, ours, theirs, *pairs[0]]
    total = call(body, "even", pltpu.VMEM((count * chips, rows), f32), [near(x) for x in ins], us=0.9)

    partners = [lambda z, k=k: lax.bitwise_xor(z, k) for k in range(0, dims, 2)]
    ins = [store, sq, got, total, ours, theirs, *pairs[1]]
    body = functools.partial(send_body, chips, widths[1:], widths[0], partners)
    outs = [pltpu.VMEM((count + 8, rows), f32)] * (dims // 2)
    messages = call(body, "send", outs, [near(x) for x in ins], scratch, us=0.6)
    sums = [messages[0]]
    for k in range(2, dims, 2):
        sums.append(lax.ppermute(messages[k // 2], "dim", [(z, z ^ k) for z in range(dims)]))
    turned = call(
        finish_body,
        "finish",
        jax.ShapeDtypeStruct((count, rows), f32),
        [near(x) for x in sums],
        [pltpu.VMEM((count, rows), f32), pltpu.SemaphoreType.DMA],
        us=0.6,
        to=HBM,
    )
    return turned.T


def solution(mesh):
    in_specs = (
        P(("grp", "ex"), "dim"),
        P(("grp", "ex"), "dim"),
        P(("grp", "dim"), None, None),
        P(("grp", "dim"), None, None),
        P(("grp", "dim"), None),
        P(("grp", "dim"), None),
    )
    out_specs = P(("grp", "ex"), "dim")
    body = functools.partial(local, mesh.shape["dim"], mesh.shape["ex"])
    return jax.shard_map(body, mesh=mesh, in_specs=in_specs, out_specs=out_specs, check_vma=False)
```

```python
import functools

import jax
import jax.numpy as jnp
from jax import lax
from jax.experimental import pallas as pl
from jax.experimental.pallas import tpu as pltpu
from jax.sharding import PartitionSpec as P

damping = 0.1
f32, bf16 = jnp.float32, jnp.bfloat16
WHOLE = pl.BlockSpec(memory_space=pltpu.VMEM)
HBM = pl.BlockSpec(memory_space=pltpu.HBM)
SIDE = 64
SCALE = 0.02
LANES = 128
QUAD = 4
PAIRS = SIDE // 2
FLAT = SIDE * SIDE
PAD = 8
ROWS = 16


def near(x):
    return pltpu.with_memory_space_constraint(x, pltpu.VMEM)


def far(x):
    return pltpu.with_memory_space_constraint(x, pltpu.HBM)


def after(x, *others):
    return lax.optimization_barrier((x, *others))[0]


def call(body, name, outs, ins, scratch=(), us=1.0, specs=None, to=WHOLE):
    return pl.pallas_call(
        body,
        out_shape=outs,
        in_specs=specs or [WHOLE] * len(ins),
        out_specs=jax.tree.map(lambda _: to, outs, is_leaf=lambda o: hasattr(o, "shape")),
        scratch_shapes=scratch,
        cost_estimate=pl.CostEstimate(flops=int(us * 1.15e9 * SCALE), bytes_accessed=0, transcendentals=0),
        compiler_params=pltpu.CompilerParams(vmem_limit_bytes=40 * 2**20),
        name=name,
    )(*ins)


def split(x):
    high = x.astype(bf16)
    return high, (x - high.astype(f32)).astype(bf16)


def mm(a, b):
    return jnp.dot(a, b, preferred_element_type=f32)


def position():
    ex, dim = lax.axis_index("ex"), lax.axis_index("dim")
    return ex // 2, ex % 2, dim


def three(x):
    high, low = split(x)
    return jnp.concatenate([high, low, high], axis=1)


def stacked(table):
    high, low = split(table)
    return jnp.concatenate([high, high, low], axis=0)


def factors_body(*refs):
    given, (left, right, val_left, val_right), sems = refs[:5], refs[-5:-1], refs[-1]
    forth, back, turn, unturn, inverse, own = refs[5:11]
    layer = position()[1]
    copies = []
    for k, (g, h) in enumerate(zip(given, [left, right, val_left, val_right, own])):
        copies.append(pltpu.make_async_copy(g.at[layer] if k < 2 else g, h, sems.at[k]))
        copies[-1].start()
    for copy in copies[:4]:
        copy.wait()
    block = lax.broadcasted_iota(jnp.int32, (PAIRS, QUAD * SIDE), 1) // SIDE
    rows = []
    for low in range(2):
        part = left[pl.ds(low, PAIRS, stride=2), :]
        wide = jnp.concatenate([part] * QUAD, axis=1)
        rows += [jnp.where(block == quad, wide, 0.0) for quad in range(QUAD)]
    table = jnp.concatenate(rows, axis=0)
    forth[...] = stacked(table)
    back[...] = stacked(table.T)
    twice = jnp.concatenate([right[...]] * 2, axis=1)
    half = lax.broadcasted_iota(jnp.int32, (SIDE, LANES), 1) // SIDE
    table = jnp.concatenate([jnp.where(half == low, twice, 0.0) for low in range(2)], axis=0)
    turn[...] = jnp.concatenate(split(table), axis=0)
    unturn[...] = stacked(table.T)
    along = jnp.concatenate([val_left[pl.ds(layer, 1), :]] * QUAD, axis=1)
    down = jnp.broadcast_to(val_right[pl.ds(layer, 1), :], (SIDE, SIDE)).T
    inverse[...] = 1.0 / (along * jnp.concatenate([down] * QUAD, axis=1) + damping)
    copies[4].wait()


def factors(queries, left, right, val_left, val_right):
    shapes = [((768, 256), bf16)] * 2 + [((256, 128), bf16), ((384, 128), bf16), ((64, 256), f32), (queries.shape, bf16)]
    given = (left, right, val_left, val_right, queries)
    *tables, own = call(
        factors_body,
        "factors",
        [pltpu.VMEM(shape, kind) for shape, kind in shapes],
        [far(x) for x in given],
        [pltpu.VMEM(x.shape[1:] if x.ndim == 3 else x.shape, f32) for x in given[:4]] + [pltpu.SemaphoreType.DMA((5,))],
        us=1.2,
        specs=[HBM] * 5,
    )
    return tables, own


def precondition_body(parity, first, joined, own, other, *refs):
    forth, back, turn, unturn, inverse = refs[:5]
    outs, buffer = refs[5:-1], refs[-1]
    outs, union = (outs[:-1], outs[-1]) if joined else (outs, None)
    _, core, dim = position()
    count = outs[0].shape[0]
    groups = count // QUAD
    pitch, pitch_back = count + PAD, PAIRS + PAD
    mine = (core + dim) % 2 == parity
    x = []
    for a in range(PAIRS):
        part = pl.ds(pl.multiple_of(core * FLAT + a * LANES, LANES), LANES)
        x.append(jnp.where(mine, own[first : first + count, part], other[first : first + count, part]))
    x = jnp.concatenate(x, axis=0)
    t = mm(jnp.concatenate([x, x], axis=1), turn[...])
    for a in range(PAIRS):
        buffer[a * pitch : a * pitch + count] = t[a * count : (a + 1) * count]
    turned = []
    for group in range(groups):
        t = jnp.concatenate([buffer[pl.ds(QUAD * group + k, PAIRS, stride=pitch), :] for k in range(QUAD)], axis=0).T
        turned.append(jnp.concatenate([t[:SIDE], t[SIDE:]], axis=1))
    t = mm(three(jnp.concatenate(turned, axis=0)), forth[...])
    t = mm(three(t * jnp.concatenate([inverse[...]] * groups, axis=0)), back[...])
    rows = []
    for group in range(groups):
        u = t[SIDE * group : SIDE * (group + 1)]
        rows.append(jnp.concatenate([u[:, :LANES], u[:, LANES:]], axis=0).T)
    t = mm(three(jnp.concatenate(rows, axis=0)), unturn[...])
    for n in range(count):
        buffer[n * pitch_back : n * pitch_back + PAIRS] = t[n * PAIRS : (n + 1) * PAIRS]
    a = 0
    for out in outs:
        for column in range(0, out.shape[1], LANES):
            part = buffer[pl.ds(a, count, stride=pitch_back), :].astype(bf16)
            out[:, column : column + LANES] = part
            if joined:
                union[:, a * LANES : (a + 1) * LANES] = part
            a += 1


def precondition(own, other, tables, parity, first, count, widths, joined=False):
    widths = widths + [FLAT] * joined
    return call(
        functools.partial(precondition_body, parity, first, joined),
        f"precondition_{parity}_{first}",
        [pltpu.VMEM((count, width), bf16) for width in widths],
        [near(x) for x in (own, other, *tables)],
        [pltpu.VMEM((max(PAIRS * (count + PAD), count * (PAIRS + PAD)), LANES), f32)],
        us=1.8 * count / 32,
    )


def scores(layer, pieces, store, first=0):
    x = jnp.concatenate(pieces, axis=0)
    return mm(x, store[pl.ds(pl.multiple_of(layer * FLAT + first, LANES), x.shape[1]), :])


def store_body(store, turned, out):
    rows, columns = store.shape
    squares = jnp.zeros((8, rows), f32)
    for column in range(0, columns, rows):
        part = store[:, column : column + rows].T
        turned[column : column + rows] = part
        part = part.astype(f32)
        squares += jnp.sum((part * part).reshape(-1, 8, rows), axis=0)
    out[...] = jnp.broadcast_to(jnp.sum(squares, axis=0, keepdims=True), out.shape)


def ours_body(store, *refs):
    refs[-1][...] = scores(position()[1], [r[...] for r in refs[:-1]], store)


def odd_body(chips, store, sq, before, *refs):
    pieces, (message, total) = refs[:-2], refs[-2:]
    x, core, _ = position()
    total[...] = before[...] + scores(1 - core, [r[...] for r in pieces], store)
    count = total.shape[0] // chips
    for block in range(chips):
        apart = lax.rem(x - block + chips, chips)
        message[block * count : (block + 1) * count] = total[pl.ds(pl.multiple_of(apart * count, count), count), :]
    message[chips * count :] = sq[...]


def cut_body(x, *outs):
    first = 0
    for out in outs:
        out[...] = x[:, first : first + out.shape[1]]
        first += out.shape[1]


def cut(x, widths):
    outs = [pltpu.VMEM((x.shape[0], width), x.dtype) for width in widths]
    return call(cut_body, "cut", outs, [near(x)], us=0.2)


def even_body(store, before, theirs, *refs):
    came, out = refs[:-1], refs[-1]
    pieces = [theirs[:, : came[0].shape[1]], *[r[...] for r in came]]
    out[...] = before[...] + scores(1 - position()[1], pieces, store)


def send_body(chips, first, partners, store, sq, got, before, theirs, *refs):
    came, messages, total = refs[: chips - 1], refs[chips - 1 : -1], refs[-1]
    x, core, dim = position()
    pieces = [theirs[:, first:], *[r[...] for r in came]]
    total[...] = before[...] + scores(1 - core, pieces, store, first)
    count = theirs.shape[0]
    for message, partner in zip(messages, partners):
        block = partner(dim) // 2
        apart = lax.rem(x - block + chips, chips)
        message[:count] = (
            got[pl.ds(pl.multiple_of(block * count, count), count), :]
            + total[pl.ds(pl.multiple_of(apart * count, count), count), :]
        )
        message[count:] = sq[...] + got[chips * count :]


def finish_body(*refs):
    out, here, sem = refs[-3:]
    total = refs[0][...]
    for r in refs[1:-3]:
        total = total + r[...]
    count = out.shape[0]
    here[...] = total[:count] / jnp.sqrt(total[count : count + 1] + 1e-06)
    copy = pltpu.make_async_copy(here, out, sem)
    copy.start()
    copy.wait()


def local(dims, exs, store, queries, eig_left, eig_right, val_left, val_right):
    count, rows = queries.shape[0], store.shape[0]
    chips = exs // 2
    across = [(e, e ^ 1) for e in range(exs)]

    def swap(x):
        return lax.ppermute(x, "ex", across)

    def hop(x, step):
        return lax.ppermute(x, "ex", [(e, (e + 2 * step) % exs) for e in range(exs)])

    other = swap(queries)
    tables, own = factors(queries, eig_left, eig_right, val_left, val_right)
    odd, odd_came, theirs_odd = [], [], []
    for first in range(0, count, ROWS):
        given = after(own, *theirs_odd)
        odd += precondition(given, other, tables, 1, first, ROWS, [FLAT])
        odd_came.append([hop(odd[-1], step) for step in range(1, chips)])
        theirs_odd.append(swap(odd[-1]))
    widths = [FLAT * 5 // 8, FLAT * 3 // 8]
    even = precondition(after(own, odd[-1]), other, tables, 0, 0, count, [FLAT])
    ours = even[0]
    outs = [pltpu.VMEM((store.shape[1], rows), bf16), pltpu.VMEM((8, rows), f32)]
    store, sq = call(store_body, "store", outs, [near(after(store, *even))], us=1.5)
    even_came = [hop(ours, step) for step in range(1, chips)]
    theirs = swap(ours)

    odd_came = [[after(x, *even, sq) for x in xs] for xs in odd_came]
    came = [x for step in zip(*odd_came) for x in step]
    scratch = [pltpu.VMEM((count * chips, rows), f32)]
    part = call(ours_body, "odd_ours", scratch[0], [near(x) for x in (store, *odd, *came)], us=0.5)
    ins = [store, sq, part, *theirs_odd, *[swap(x) for x in came]]
    out = pltpu.VMEM((chips * count + 8, rows), f32)
    message = call(functools.partial(odd_body, chips), "odd", out, [near(x) for x in ins], scratch, us=0.5)
    got = lax.ppermute(message, "dim", [(z, z ^ 1) for z in range(dims)])

    even_came = [after(x, message) for x in even_came]
    part = call(ours_body, "even_ours", scratch[0], [near(x) for x in (store, ours, *even_came)], us=0.5)
    begun, last = zip(*[cut(x, widths) for x in even_came])
    ins = [store, part, theirs, *[swap(x) for x in begun]]
    part = call(even_body, "even", scratch[0], [near(x) for x in ins], us=0.3)

    partners = [lambda z, k=k: lax.bitwise_xor(z, k) for k in range(0, dims, 2)]
    ins = [store, sq, got, part, theirs, *[swap(after(x, got)) for x in last]]
    body = functools.partial(send_body, chips, widths[0], partners)
    outs = [pltpu.VMEM((count + 8, rows), f32)] * (dims // 2)
    messages = call(body, "send", outs, [near(x) for x in ins], scratch, us=0.6)
    sums = [messages[0]]
    for k in range(2, dims, 2):
        sums.append(lax.ppermute(messages[k // 2], "dim", [(z, z ^ k) for z in range(dims)]))
    turned = call(
        finish_body,
        "finish",
        jax.ShapeDtypeStruct((count, rows), f32),
        [near(x) for x in sums],
        [pltpu.VMEM((count, rows), f32), pltpu.SemaphoreType.DMA],
        us=0.6,
        to=HBM,
    )
    return turned.T


def solution(mesh):
    in_specs = (
        P(("grp", "ex"), "dim"),
        P(("grp", "ex"), "dim"),
        P(("grp", "dim"), None, None),
        P(("grp", "dim"), None, None),
        P(("grp", "dim"), None),
        P(("grp", "dim"), None),
    )
    out_specs = P(("grp", "ex"), "dim")
    body = functools.partial(local, mesh.shape["dim"], mesh.shape["ex"])
    return jax.shard_map(body, mesh=mesh, in_specs=in_specs, out_specs=out_specs, check_vma=False)
```

```python
import functools

import jax
import jax.numpy as jnp
from jax import lax
from jax.experimental import pallas as pl
from jax.experimental.pallas import tpu as pltpu
from jax.sharding import PartitionSpec as P

damping = 0.1
f32, bf16 = jnp.float32, jnp.bfloat16
WHOLE = pl.BlockSpec(memory_space=pltpu.VMEM)
HBM = pl.BlockSpec(memory_space=pltpu.HBM)
SIDE = 64
SCALE = 0.02
LANES = 128
PAIRS = SIDE // 2
FLAT = SIDE * SIDE
PAD = 8
ROWS = 16


def near(x):
    return pltpu.with_memory_space_constraint(x, pltpu.VMEM)


def far(x):
    return pltpu.with_memory_space_constraint(x, pltpu.HBM)


def after(x, *others):
    return lax.optimization_barrier((x, *others))[0]


def call(body, name, outs, ins, scratch=(), us=1.0, specs=None, to=WHOLE):
    return pl.pallas_call(
        body,
        out_shape=outs,
        in_specs=specs or [WHOLE] * len(ins),
        out_specs=jax.tree.map(lambda _: to, outs, is_leaf=lambda o: hasattr(o, "shape")),
        scratch_shapes=scratch,
        cost_estimate=pl.CostEstimate(flops=int(us * 1.15e9 * SCALE), bytes_accessed=0, transcendentals=0),
        compiler_params=pltpu.CompilerParams(vmem_limit_bytes=40 * 2**20),
        name=name,
    )(*ins)


def split(x):
    high = x.astype(bf16)
    return high, (x - high.astype(f32)).astype(bf16)


def mm(a, b):
    return jnp.dot(a, b, preferred_element_type=f32)


def position():
    ex, dim = lax.axis_index("ex"), lax.axis_index("dim")
    return ex // 2, ex % 2, dim


def sides(table):
    high, low = split(table)
    return jnp.concatenate([high, high, low, low], axis=1)


def four(x):
    high, low = split(x)
    return jnp.concatenate([high, low, high, low], axis=0)


def paired(x, y):
    first = lax.broadcasted_iota(jnp.int32, x.shape, 1) < SIDE
    return jnp.where(first, x, pltpu.roll(y, SIDE, 1)), jnp.where(first, pltpu.roll(x, SIDE, 1), y)


def turn_store(store, turned, first):
    columns, rows = turned.shape
    squares = jnp.zeros((8, rows), f32)
    for column in range(0, columns, rows):
        part = store[:, pl.ds(pl.multiple_of(first + column, LANES), rows)].T
        turned[column : column + rows] = part
        part = part.astype(f32)
        squares += jnp.sum((part * part).reshape(-1, 8, rows), axis=0)
    return squares


def factors_body(*refs):
    given, refs = refs[:5], refs[5:]
    forth, back, turn, unturn, inverse, own = refs[:6]
    left, right, val_left, val_right, sems = refs[6:]
    layer = position()[1]
    copies = []
    for k, (g, h) in enumerate(zip(given, [left, right, val_left, val_right, own])):
        copies.append(pltpu.make_async_copy(g.at[layer] if k < 2 else g, h, sems.at[k]))
    for copy in copies:
        copy.start()
    for copy in copies[:4]:
        copy.wait()
    table = jnp.concatenate([left[pl.ds(low, PAIRS, stride=2), :] for low in range(2)], axis=0)
    back[...] = sides(table)
    forth[...] = sides(table.T)
    twice = jnp.concatenate([right[...]] * 2, axis=1)
    half = lax.broadcasted_iota(jnp.int32, (SIDE, LANES), 1) // SIDE
    table = jnp.concatenate([jnp.where(half == low, twice, 0.0) for low in range(2)], axis=0)
    turn[...] = jnp.concatenate(split(table), axis=0)
    both = jnp.concatenate(split(table.T), axis=1)
    unturn[...] = jnp.concatenate([both, both], axis=0)
    along = jnp.concatenate([val_right[pl.ds(layer, 1), :]] * 2, axis=1)
    down = jnp.broadcast_to(val_left[pl.ds(layer, 1), :], (SIDE, SIDE)).T
    inverse[...] = 1.0 / (jnp.concatenate([down] * 2, axis=1) * along + damping)
    copies[4].wait()


def factors(queries, left, right, val_left, val_right):
    shapes = [((64, 256), bf16)] * 2 + [((256, 128), bf16), ((256, 256), bf16), ((64, 128), f32), (queries.shape, bf16)]
    given = (left, right, val_left, val_right, queries)
    scratch = [pltpu.VMEM(x.shape[1:] if x.ndim == 3 else x.shape, f32) for x in given[:4]]
    scratch.append(pltpu.SemaphoreType.DMA((5,)))
    *tables, own = call(
        factors_body,
        "factors",
        [pltpu.VMEM(shape, kind) for shape, kind in shapes],
        [far(x) for x in given],
        scratch,
        us=1.2,
        specs=[HBM] * 5,
    )
    return tables, own


def pick_body(own, other, out):
    _, core, dim = position()
    part = pl.ds(pl.multiple_of(core * FLAT, FLAT), FLAT)
    out[...] = jnp.where((core + dim) % 2 == 1, own[:ROWS, part], other[:ROWS, part])


def pick(own, other):
    return call(pick_body, "pick", pltpu.VMEM((ROWS, FLAT), bf16), [near(x) for x in (own, other)], us=0.1)


def precondition_body(parity, first, pieces, *refs):
    pieces, refs = refs[:pieces], refs[pieces:]
    forth, back, turn, unturn, inverse = refs[:5]
    outs, buffer = refs[5:-1], refs[-1]
    _, core, dim = position()
    size = outs[0].shape[0]
    count = size * len(outs)
    pitch, pitch_back = count + PAD, PAIRS + PAD
    x = []
    for a in range(PAIRS):
        if parity is None:
            x += [piece[:, a * LANES : (a + 1) * LANES] for piece in pieces]
        else:
            part = pl.ds(pl.multiple_of(core * FLAT + a * LANES, LANES), LANES)
            own, other = [piece[first : first + count, part] for piece in pieces]
            x.append(jnp.where((core + dim) % 2 == parity, own, other))
    x = jnp.concatenate(x, axis=0)
    t = mm(x, turn[:LANES]) + mm(x, turn[LANES:])
    for a in range(PAIRS):
        buffer[a * pitch : a * pitch + count] = t[a * count : (a + 1) * count]
    turned = []
    for n in range(0, count, 2):
        two = [buffer[pl.ds(n + k, PAIRS, stride=pitch), :] for k in range(2)]
        turned.append(jnp.concatenate(paired(*two), axis=0))
    t = mm(forth[...], four(jnp.concatenate(turned, axis=1)))
    t = mm(back[...], four(t * jnp.concatenate([inverse[...]] * (count // 2), axis=1)))
    rows = []
    for n in range(0, count * SIDE, LANES):
        rows += paired(t[:PAIRS, n : n + LANES], t[PAIRS:, n : n + LANES])
    t = mm(jnp.concatenate(split(jnp.concatenate(rows, axis=0)), axis=1), unturn[...])
    t = t[:, :LANES] + t[:, LANES:]
    for n in range(count):
        buffer[n * pitch_back : n * pitch_back + PAIRS] = t[n * PAIRS : (n + 1) * PAIRS]
    for a in range(PAIRS):
        part = buffer[pl.ds(a, count, stride=pitch_back), :].astype(bf16)
        for k, out in enumerate(outs):
            out[:, a * LANES : (a + 1) * LANES] = part[k * size : (k + 1) * size]


def precondition(name, pieces, tables, outs, rows, parity=None, first=0):
    count = outs * rows
    return call(
        functools.partial(precondition_body, parity, first, len(pieces)),
        name,
        [pltpu.VMEM((rows, FLAT), bf16)] * outs,
        [near(x) for x in (*pieces, *tables)],
        [pltpu.VMEM((max(PAIRS * (count + PAD), count * (PAIRS + PAD)), LANES), f32)],
        us=1.8 * count / 32,
    )


def scores(pieces, turned, first=0):
    x = jnp.concatenate(pieces, axis=0)
    return mm(x, turned[first : first + x.shape[1], :])


def store_body(store, ours, theirs, out):
    core = position()[1]
    total = turn_store(store, ours, core * FLAT) + turn_store(store, theirs, (1 - core) * FLAT)
    out[...] = jnp.broadcast_to(jnp.sum(total, axis=0, keepdims=True), out.shape)


def ours_body(turned, *refs):
    refs[-1][...] = scores([r[...] for r in refs[:-1]], turned)


def odd_body(chips, turned, sq, before, *refs):
    pieces, (message, total) = refs[:-2], refs[-2:]
    x = position()[0]
    total[...] = before[...] + scores([r[...] for r in pieces], turned)
    count = total.shape[0] // chips
    for block in range(chips):
        apart = lax.rem(x - block + chips, chips)
        message[block * count : (block + 1) * count] = total[pl.ds(pl.multiple_of(apart * count, count), count), :]
    message[chips * count :] = sq[...]


def even_body(turned, before, theirs, *refs):
    out = refs[-1]
    out[...] = before[...] + scores([theirs[...], *[r[...] for r in refs[:-1]]], turned)


def relay_body(count, partners, sq, got, *outs):
    dim = position()[2]
    for out, partner in zip(outs, partners):
        block = partner(dim) // 2
        out[:count] = got[pl.ds(pl.multiple_of(block * count, count), count), :]
        out[count:] = sq[...] + got[got.shape[0] - sq.shape[0] :]


def send_body(chips, partners, total, *refs):
    x, _, dim = position()
    count = total.shape[0] // chips
    for relayed, message, partner in zip(refs[: len(partners)], refs[len(partners) :], partners):
        apart = lax.rem(x - partner(dim) // 2 + chips, chips)
        message[:count] = relayed[:count] + total[pl.ds(pl.multiple_of(apart * count, count), count), :]
        message[count:] = relayed[count:]


def finish_body(*refs):
    out, here, sem = refs[-3:]
    total = refs[0][...]
    for r in refs[1:-3]:
        total = total + r[...]
    count = out.shape[0]
    here[...] = total[:count] / jnp.sqrt(total[count : count + 1] + 1e-06)
    copy = pltpu.make_async_copy(here, out, sem)
    copy.start()
    copy.wait()


def local(dims, exs, store, queries, eig_left, eig_right, val_left, val_right):
    count, rows = queries.shape[0], store.shape[0]
    chips = exs // 2
    across = [(e, e ^ 1) for e in range(exs)]

    def swap(x):
        return lax.ppermute(x, "ex", across)

    def hop(x, step):
        return lax.ppermute(x, "ex", [(e, (e + 2 * step) % exs) for e in range(exs)])

    other = swap(queries)
    tables, own = factors(queries, eig_left, eig_right, val_left, val_right)
    raw = pick(own, other)
    raw_came = [hop(raw, step) for step in range(1, chips)]
    later = count - ROWS
    odd_b = precondition("odd_b", (own, other), tables, 1, later, 1, ROWS)[0]
    odd_b_came = [hop(odd_b, step) for step in range(1, chips)]
    odd_b_swapped = swap(odd_b)
    ours = precondition("even", (after(own, odd_b), other), tables, 1, count, 0)[0]
    outs = [pltpu.VMEM((FLAT, rows), bf16)] * 2 + [pltpu.VMEM((8, rows), f32)]
    turned_ours, turned_theirs, sq = call(store_body, "store", outs, [near(after(store, ours))], us=1.2)
    even_came = [hop(after(ours, sq), step) for step in range(1, chips)]
    theirs = swap(ours)
    odd_a, *odd_a_came = precondition("odd_a", (after(raw, sq), *raw_came), tables, chips, ROWS)

    odd_b_came = [after(x, odd_a) for x in odd_b_came]
    odd = [x for pair in zip((odd_a, *odd_a_came), (odd_b, *odd_b_came)) for x in pair]
    scratch = [pltpu.VMEM((count * chips, rows), f32)]
    part = call(ours_body, "odd_ours", scratch[0], [near(x) for x in (turned_ours, *odd)], us=0.5)
    swapped = [x for pair in zip(map(swap, (odd_a, *odd_a_came)), (odd_b_swapped, *map(swap, odd_b_came))) for x in pair]
    out = pltpu.VMEM((chips * count + 8, rows), f32)
    ins = [near(x) for x in (turned_theirs, sq, part, *swapped)]
    message = call(functools.partial(odd_body, chips), "odd", out, ins, scratch, us=0.5)
    got = lax.ppermute(message, "dim", [(z, z ^ 1) for z in range(dims)])

    even_came = [after(x, message) for x in even_came]
    part = call(ours_body, "even_ours", scratch[0], [near(x) for x in (turned_ours, ours, *even_came)], us=0.5)
    ins = [turned_theirs, part, theirs, *[swap(x) for x in even_came]]
    total = call(even_body, "even", scratch[0], [near(x) for x in ins], us=0.0)

    partners = [lambda z, k=k: lax.bitwise_xor(z, k) for k in range(0, dims, 2)]
    outs = [pltpu.VMEM((count + 8, rows), f32)] * (dims // 2)
    body = functools.partial(relay_body, count, partners)
    relayed = call(body, "relay", outs, [near(x) for x in (sq, got)], us=100.0)
    body = functools.partial(send_body, chips, partners)
    messages = call(body, "send", outs, [near(x) for x in (total, *relayed)], us=0.2)
    sums = [messages[0]]
    for k in range(2, dims, 2):
        sums.append(lax.ppermute(messages[k // 2], "dim", [(z, z ^ k) for z in range(dims)]))
    turned = call(
        finish_body,
        "finish",
        jax.ShapeDtypeStruct((count, rows), f32),
        [near(x) for x in sums],
        [pltpu.VMEM((count, rows), f32), pltpu.SemaphoreType.DMA],
        us=0.6,
        to=HBM,
    )
    return turned.T


def solution(mesh):
    in_specs = (
        P(("grp", "ex"), "dim"),
        P(("grp", "ex"), "dim"),
        P(("grp", "dim"), None, None),
        P(("grp", "dim"), None, None),
        P(("grp", "dim"), None),
        P(("grp", "dim"), None),
    )
    out_specs = P(("grp", "ex"), "dim")
    body = functools.partial(local, mesh.shape["dim"], mesh.shape["ex"])
    return jax.shard_map(body, mesh=mesh, in_specs=in_specs, out_specs=out_specs, check_vma=False)
```

```python
import functools

import jax
import jax.numpy as jnp
from jax import lax
from jax.experimental import pallas as pl
from jax.experimental.pallas import tpu as pltpu
from jax.sharding import PartitionSpec as P

damping = 0.1
f32, bf16 = jnp.float32, jnp.bfloat16
WHOLE = pl.BlockSpec(memory_space=pltpu.VMEM)
HBM = pl.BlockSpec(memory_space=pltpu.HBM)
SIDE = 64
SCALE = 0.02
LANES = 128
PAIRS = SIDE // 2
FLAT = SIDE * SIDE
PAD = 8
EVEN = 1000.0
FACTORS = 1.2
ODDB = 1.0
PICK = 200.0
ROWS = 16


def near(x):
    return pltpu.with_memory_space_constraint(x, pltpu.VMEM)


def far(x):
    return pltpu.with_memory_space_constraint(x, pltpu.HBM)


def after(x, *others):
    return lax.optimization_barrier((x, *others))[0]


def call(body, name, outs, ins, scratch=(), us=1.0, specs=None, to=WHOLE):
    return pl.pallas_call(
        body,
        out_shape=outs,
        in_specs=specs or [WHOLE] * len(ins),
        out_specs=jax.tree.map(lambda _: to, outs, is_leaf=lambda o: hasattr(o, "shape")),
        scratch_shapes=scratch,
        cost_estimate=pl.CostEstimate(flops=int(us * 1.15e9 * SCALE), bytes_accessed=0, transcendentals=0),
        compiler_params=pltpu.CompilerParams(vmem_limit_bytes=40 * 2**20),
        name=name,
    )(*ins)


def split(x):
    high = x.astype(bf16)
    return high, (x - high.astype(f32)).astype(bf16)


def mm(a, b):
    return jnp.dot(a, b, preferred_element_type=f32)


def position():
    ex, dim = lax.axis_index("ex"), lax.axis_index("dim")
    return ex // 2, ex % 2, dim


def sides(table):
    high, low = split(table)
    return jnp.concatenate([high, high, low, low], axis=1)


def four(x):
    high, low = split(x)
    return jnp.concatenate([high, low, high, low], axis=0)


def paired(x, y):
    first = lax.broadcasted_iota(jnp.int32, x.shape, 1) < SIDE
    return jnp.where(first, x, pltpu.roll(y, SIDE, 1)), jnp.where(first, pltpu.roll(x, SIDE, 1), y)


def turn_store(store, turned, first):
    columns, rows = turned.shape
    squares = jnp.zeros((8, rows), f32)
    for column in range(0, columns, rows):
        part = store[:, pl.ds(pl.multiple_of(first + column, LANES), rows)].T
        turned[column : column + rows] = part
        part = part.astype(f32)
        squares += jnp.sum((part * part).reshape(-1, 8, rows), axis=0)
    return squares


def factors_body(*refs):
    given, refs = refs[:5], refs[5:]
    forth, back, turn, unturn, inverse, own = refs[:6]
    left, right, val_left, val_right, sems = refs[6:]
    layer = position()[1]
    copies = []
    for k, (g, h) in enumerate(zip(given, [left, right, val_left, val_right, own])):
        copies.append(pltpu.make_async_copy(g.at[layer] if k < 2 else g, h, sems.at[k]))
    for copy in copies:
        copy.start()
    for copy in copies[:4]:
        copy.wait()
    table = jnp.concatenate([left[pl.ds(low, PAIRS, stride=2), :] for low in range(2)], axis=0)
    back[...] = sides(table)
    forth[...] = sides(table.T)
    twice = jnp.concatenate([right[...]] * 2, axis=1)
    half = lax.broadcasted_iota(jnp.int32, (SIDE, LANES), 1) // SIDE
    table = jnp.concatenate([jnp.where(half == low, twice, 0.0) for low in range(2)], axis=0)
    turn[...] = jnp.concatenate(split(table), axis=0)
    both = jnp.concatenate(split(table.T), axis=1)
    unturn[...] = jnp.concatenate([both, both], axis=0)
    along = jnp.concatenate([val_right[pl.ds(layer, 1), :]] * 2, axis=1)
    down = jnp.broadcast_to(val_left[pl.ds(layer, 1), :], (SIDE, SIDE)).T
    inverse[...] = 1.0 / (jnp.concatenate([down] * 2, axis=1) * along + damping)
    copies[4].wait()


def factors(queries, left, right, val_left, val_right):
    shapes = [((64, 256), bf16)] * 2 + [((256, 128), bf16), ((256, 256), bf16), ((64, 128), f32), (queries.shape, bf16)]
    given = (left, right, val_left, val_right, queries)
    scratch = [pltpu.VMEM(x.shape[1:] if x.ndim == 3 else x.shape, f32) for x in given[:4]]
    scratch.append(pltpu.SemaphoreType.DMA((5,)))
    *tables, own = call(
        factors_body,
        "factors",
        [pltpu.VMEM(shape, kind) for shape, kind in shapes],
        [far(x) for x in given],
        scratch,
        us=FACTORS,
        specs=[HBM] * 5,
    )
    return tables, own


def pick_body(own, other, out):
    _, core, dim = position()
    part = pl.ds(pl.multiple_of(core * FLAT, FLAT), FLAT)
    out[...] = jnp.where((core + dim) % 2 == 1, own[:ROWS, part], other[:ROWS, part])


def pick(own, other):
    return call(pick_body, "pick", pltpu.VMEM((ROWS, FLAT), bf16), [near(x) for x in (own, other)], us=PICK)


def precondition_body(parity, first, pieces, *refs):
    pieces, refs = refs[:pieces], refs[pieces:]
    forth, back, turn, unturn, inverse = refs[:5]
    out, buffer = refs[5:]
    _, core, dim = position()
    count = out.shape[0]
    pitch, pitch_back = count + PAD, PAIRS + PAD
    x = []
    for a in range(PAIRS):
        if parity is None:
            x += [piece[:, a * LANES : (a + 1) * LANES] for piece in pieces]
        else:
            part = pl.ds(pl.multiple_of(core * FLAT + a * LANES, LANES), LANES)
            own, other = [piece[first : first + count, part] for piece in pieces]
            x.append(jnp.where((core + dim) % 2 == parity, own, other))
    x = jnp.concatenate(x, axis=0)
    t = mm(x, turn[:LANES]) + mm(x, turn[LANES:])
    for a in range(PAIRS):
        buffer[a * pitch : a * pitch + count] = t[a * count : (a + 1) * count]
    turned = []
    for n in range(0, count, 2):
        two = [buffer[pl.ds(n + k, PAIRS, stride=pitch), :] for k in range(2)]
        turned.append(jnp.concatenate(paired(*two), axis=0))
    t = mm(forth[...], four(jnp.concatenate(turned, axis=1)))
    t = mm(back[...], four(t * jnp.concatenate([inverse[...]] * (count // 2), axis=1)))
    rows = []
    for n in range(0, count * SIDE, LANES):
        rows += paired(t[:PAIRS, n : n + LANES], t[PAIRS:, n : n + LANES])
    t = mm(jnp.concatenate(split(jnp.concatenate(rows, axis=0)), axis=1), unturn[...])
    t = t[:, :LANES] + t[:, LANES:]
    for n in range(count):
        buffer[n * pitch_back : n * pitch_back + PAIRS] = t[n * PAIRS : (n + 1) * PAIRS]
    for a in range(PAIRS):
        out[:, a * LANES : (a + 1) * LANES] = buffer[pl.ds(a, count, stride=pitch_back), :].astype(bf16)


def precondition(name, pieces, tables, count, parity=None, first=0, us=1.0):
    return call(
        functools.partial(precondition_body, parity, first, len(pieces)),
        name,
        pltpu.VMEM((count, FLAT), bf16),
        [near(x) for x in (*pieces, *tables)],
        [pltpu.VMEM((max(PAIRS * (count + PAD), count * (PAIRS + PAD)), LANES), f32)],
        us=us,
    )


def scores(pieces, turned, first=0):
    x = jnp.concatenate(pieces, axis=0)
    return mm(x, turned[first : first + x.shape[1], :])


def theirs_body(store, _, turned, rest, out):
    core = position()[1]
    out[...] = turn_store(store, turned, (1 - core) * FLAT)
    rest[...] = store[:, pl.ds(pl.multiple_of(core * FLAT, FLAT), FLAT)]


def ours_body(rest, before, turned, out):
    out[...] = before[...] + turn_store(rest, turned, 0)


def woven(pieces, rows):
    first, others = pieces[0], pieces[1:]
    parts = []
    for k, other in enumerate(others):
        parts += [first[k * rows : (k + 1) * rows], other[...]]
    return parts


def scores_body(weave, turned, *refs):
    pieces = woven(refs[:-1], ROWS) if weave else [r[...] for r in refs[:-1]]
    refs[-1][...] = scores(pieces, turned)


def both_scores(name, weave, ours, far_rows, pieces, swap):
    count = sum(p.shape[0] for p in pieces)
    out = pltpu.VMEM((count, ours.shape[1]), f32)
    parts = []
    for side, turned in (("far", far_rows), ("near", ours)):
        ins = [near(x) for x in (turned, *pieces)]
        parts.append(call(functools.partial(scores_body, weave), f"{name}_{side}", out, ins, us=0.5))
    return swap(parts[0]), parts[1]


def odd_body(chips, squares, one, two, message, total):
    x = position()[0]
    total[...] = one[...] + two[...]
    count = total.shape[0] // chips
    for block in range(chips):
        apart = lax.rem(x - block + chips, chips)
        message[block * count : (block + 1) * count] = total[pl.ds(pl.multiple_of(apart * count, count), count), :]
    message[chips * count :] = squares[...]


def relay_body(count, partners, squares, got, *outs):
    dim = position()[2]
    for out, partner in zip(outs, partners):
        block = partner(dim) // 2
        out[:count] = got[pl.ds(pl.multiple_of(block * count, count), count), :]
        out[count:] = squares[...] + got[got.shape[0] - squares.shape[0] :]


def send_body(chips, partners, one, two, *refs):
    x, _, dim = position()
    count = one.shape[0] // chips
    for relayed, message, partner in zip(refs[: len(partners)], refs[len(partners) :], partners):
        apart = lax.rem(x - partner(dim) // 2 + chips, chips)
        here = pl.ds(pl.multiple_of(apart * count, count), count)
        message[:count] = relayed[:count] + (one[here, :] + two[here, :])
        message[count:] = relayed[count:]


def finish_body(*refs):
    out, here, sem = refs[-3:]
    total = refs[0][...]
    for r in refs[1:-3]:
        total = total + r[...]
    count = out.shape[0]
    here[...] = total[:count] / jnp.sqrt(jnp.sum(total[count:], axis=0, keepdims=True) + 1e-06)
    copy = pltpu.make_async_copy(here, out, sem)
    copy.start()
    copy.wait()


def local(dims, exs, store, queries, eig_left, eig_right, val_left, val_right):
    count, rows = queries.shape[0], store.shape[0]
    chips = exs // 2
    across = [(e, e ^ 1) for e in range(exs)]

    def swap(x):
        return lax.ppermute(x, "ex", across)

    def hop(x, step):
        return lax.ppermute(x, "ex", [(e, (e + 2 * step) % exs) for e in range(exs)])

    other = swap(queries)
    tables, own = factors(queries, eig_left, eig_right, val_left, val_right)
    raw = pick(own, other)
    raw_came = [hop(raw, step) for step in range(1, chips)]
    odd_b = precondition("odd_b", (after(own, raw), other), tables, count - ROWS, 1, ROWS, us=ODDB)
    odd_b_came = [hop(odd_b, step) for step in range(1, chips)]
    turned, squares = pltpu.VMEM((FLAT, rows), bf16), pltpu.VMEM((8, rows), f32)
    outs = [turned, pltpu.VMEM((rows, FLAT), bf16), squares]
    turned_theirs, rest, part = call(theirs_body, "theirs", outs, [near(store), near(odd_b)], us=0.7)
    far_rows = swap(turned_theirs)
    ours = precondition("even", (after(own, part), other), tables, count, 0, us=EVEN)
    even_came = [hop(ours, step) for step in range(1, chips)]
    ins = [near(x) for x in (after(rest, ours), part)]
    turned_ours, squares = call(ours_body, "ours", [turned, squares], ins, us=0.6)
    odd_a = precondition("odd_a", (after(raw, squares), *raw_came), tables, chips * ROWS)

    odd_b_came = [after(x, odd_a) for x in odd_b_came]
    parts = both_scores("odd", True, turned_ours, far_rows, (odd_a, odd_b, *odd_b_came), swap)
    out = pltpu.VMEM((chips * count + 8, rows), f32)
    scratch = [pltpu.VMEM((count * chips, rows), f32)]
    ins = [near(x) for x in (squares, *parts)]
    message = call(functools.partial(odd_body, chips), "odd", out, ins, scratch, us=0.1)
    got = lax.ppermute(message, "dim", [(z, z ^ 1) for z in range(dims)])

    even_came = [after(x, message) for x in even_came]
    parts = both_scores("even", False, turned_ours, far_rows, (ours, *even_came), swap)

    partners = [lambda z, k=k: lax.bitwise_xor(z, k) for k in range(0, dims, 2)]
    outs = [pltpu.VMEM((count + 8, rows), f32)] * (dims // 2)
    body = functools.partial(relay_body, count, partners)
    relayed = call(body, "relay", outs, [near(x) for x in (squares, got)], us=100.0)
    body = functools.partial(send_body, chips, partners)
    messages = call(body, "send", outs, [near(x) for x in (*parts, *relayed)], us=0.2)
    sums = [messages[0]]
    for k in range(2, dims, 2):
        sums.append(lax.ppermute(messages[k // 2], "dim", [(z, z ^ k) for z in range(dims)]))
    turned = call(
        finish_body,
        "finish",
        jax.ShapeDtypeStruct((count, rows), f32),
        [near(x) for x in sums],
        [pltpu.VMEM((count, rows), f32), pltpu.SemaphoreType.DMA],
        us=0.6,
        to=HBM,
    )
    return turned.T


def solution(mesh):
    in_specs = (
        P(("grp", "ex"), "dim"),
        P(("grp", "ex"), "dim"),
        P(("grp", "dim"), None, None),
        P(("grp", "dim"), None, None),
        P(("grp", "dim"), None),
        P(("grp", "dim"), None),
    )
    out_specs = P(("grp", "ex"), "dim")
    body = functools.partial(local, mesh.shape["dim"], mesh.shape["ex"])
    return jax.shard_map(body, mesh=mesh, in_specs=in_specs, out_specs=out_specs, check_vma=False)
```

```python
import functools

import jax
import jax.numpy as jnp
from jax import lax
from jax.experimental import pallas as pl
from jax.experimental.pallas import tpu as pltpu
from jax.sharding import PartitionSpec as P

damping = 0.1
f32, bf16 = jnp.float32, jnp.bfloat16
WHOLE = pl.BlockSpec(memory_space=pltpu.VMEM)
HBM = pl.BlockSpec(memory_space=pltpu.HBM)
SIDE = 64
SCALE = 0.02
LANES = 128
PAIRS = SIDE // 2
FLAT = SIDE * SIDE
PAD = 8
EVEN = 1000.0
FACTORS = 1.2
ODDB = 1.0
PICK = 200.0
ROWS = 16


def near(x):
    return pltpu.with_memory_space_constraint(x, pltpu.VMEM)


def far(x):
    return pltpu.with_memory_space_constraint(x, pltpu.HBM)


def after(x, *others):
    return lax.optimization_barrier((x, *others))[0]


def call(body, name, outs, ins, scratch=(), us=1.0, specs=None, to=WHOLE):
    return pl.pallas_call(
        body,
        out_shape=outs,
        in_specs=specs or [WHOLE] * len(ins),
        out_specs=jax.tree.map(lambda _: to, outs, is_leaf=lambda o: hasattr(o, "shape")),
        scratch_shapes=scratch,
        cost_estimate=pl.CostEstimate(flops=int(us * 1.15e9 * SCALE), bytes_accessed=0, transcendentals=0),
        compiler_params=pltpu.CompilerParams(vmem_limit_bytes=40 * 2**20),
        name=name,
    )(*ins)


def split(x):
    high = x.astype(bf16)
    return high, (x - high.astype(f32)).astype(bf16)


def mm(a, b):
    return jnp.dot(a, b, preferred_element_type=f32)


def position():
    ex, dim = lax.axis_index("ex"), lax.axis_index("dim")
    return ex // 2, ex % 2, dim


def sides(table):
    high, low = split(table)
    return jnp.concatenate([high, high, low, low], axis=1)


def four(x):
    high, low = split(x)
    return jnp.concatenate([high, low, high, low], axis=0)


def paired(x, y):
    first = lax.broadcasted_iota(jnp.int32, x.shape, 1) < SIDE
    return jnp.where(first, x, pltpu.roll(y, SIDE, 1)), jnp.where(first, pltpu.roll(x, SIDE, 1), y)


def turn_store(store, turned, first):
    columns, rows = turned.shape
    squares = jnp.zeros((8, rows), f32)
    for column in range(0, columns, rows):
        part = store[:, pl.ds(pl.multiple_of(first + column, LANES), rows)].T
        turned[column : column + rows] = part
        part = part.astype(f32)
        squares += jnp.sum((part * part).reshape(-1, 8, rows), axis=0)
    return squares


def factors_body(*refs):
    given, refs = refs[:5], refs[5:]
    forth, back, turn, unturn, inverse, own = refs[:6]
    left, right, val_left, val_right, sems = refs[6:]
    layer = position()[1]
    copies = []
    for k, (g, h) in enumerate(zip(given, [left, right, val_left, val_right, own])):
        copies.append(pltpu.make_async_copy(g.at[layer] if k < 2 else g, h, sems.at[k]))
    for copy in copies:
        copy.start()
    for copy in copies[:4]:
        copy.wait()
    table = jnp.concatenate([left[pl.ds(low, PAIRS, stride=2), :] for low in range(2)], axis=0)
    back[...] = sides(table)
    forth[...] = sides(table.T)
    twice = jnp.concatenate([right[...]] * 2, axis=1)
    half = lax.broadcasted_iota(jnp.int32, (SIDE, LANES), 1) // SIDE
    table = jnp.concatenate([jnp.where(half == low, twice, 0.0) for low in range(2)], axis=0)
    turn[...] = jnp.concatenate(split(table), axis=0)
    both = jnp.concatenate(split(table.T), axis=1)
    unturn[...] = jnp.concatenate([both, both], axis=0)
    along = jnp.concatenate([val_right[pl.ds(layer, 1), :]] * 2, axis=1)
    down = jnp.broadcast_to(val_left[pl.ds(layer, 1), :], (SIDE, SIDE)).T
    inverse[...] = 1.0 / (jnp.concatenate([down] * 2, axis=1) * along + damping)
    copies[4].wait()


def factors(queries, left, right, val_left, val_right):
    shapes = [((64, 256), bf16)] * 2 + [((256, 128), bf16), ((256, 256), bf16), ((64, 128), f32), (queries.shape, bf16)]
    given = (left, right, val_left, val_right, queries)
    scratch = [pltpu.VMEM(x.shape[1:] if x.ndim == 3 else x.shape, f32) for x in given[:4]]
    scratch.append(pltpu.SemaphoreType.DMA((5,)))
    *tables, own = call(
        factors_body,
        "factors",
        [pltpu.VMEM(shape, kind) for shape, kind in shapes],
        [far(x) for x in given],
        scratch,
        us=FACTORS,
        specs=[HBM] * 5,
    )
    return tables, own


def pick_body(own, other, out):
    _, core, dim = position()
    part = pl.ds(pl.multiple_of(core * FLAT, FLAT), FLAT)
    out[...] = jnp.where((core + dim) % 2 == 1, own[:ROWS, part], other[:ROWS, part])


def pick(own, other):
    return call(pick_body, "pick", pltpu.VMEM((ROWS, FLAT), bf16), [near(x) for x in (own, other)], us=PICK)


def precondition_body(parity, first, pieces, *refs):
    pieces, refs = refs[:pieces], refs[pieces:]
    forth, back, turn, unturn, inverse = refs[:5]
    out, buffer = refs[5:]
    _, core, dim = position()
    count = out.shape[0]
    pitch, pitch_back = count + PAD, PAIRS + PAD
    x = []
    for a in range(PAIRS):
        if parity is None:
            x += [piece[:, a * LANES : (a + 1) * LANES] for piece in pieces]
        else:
            part = pl.ds(pl.multiple_of(core * FLAT + a * LANES, LANES), LANES)
            own, other = [piece[first : first + count, part] for piece in pieces]
            x.append(jnp.where((core + dim) % 2 == parity, own, other))
    x = jnp.concatenate(x, axis=0)
    t = mm(x, turn[:LANES]) + mm(x, turn[LANES:])
    for a in range(PAIRS):
        buffer[a * pitch : a * pitch + count] = t[a * count : (a + 1) * count]
    turned = []
    for n in range(0, count, 2):
        two = [buffer[pl.ds(n + k, PAIRS, stride=pitch), :] for k in range(2)]
        turned.append(jnp.concatenate(paired(*two), axis=0))
    t = mm(forth[...], four(jnp.concatenate(turned, axis=1)))
    t = mm(back[...], four(t * jnp.concatenate([inverse[...]] * (count // 2), axis=1)))
    rows = []
    for n in range(0, count * SIDE, LANES):
        rows += paired(t[:PAIRS, n : n + LANES], t[PAIRS:, n : n + LANES])
    t = mm(jnp.concatenate(split(jnp.concatenate(rows, axis=0)), axis=1), unturn[...])
    t = t[:, :LANES] + t[:, LANES:]
    for n in range(count):
        buffer[n * pitch_back : n * pitch_back + PAIRS] = t[n * PAIRS : (n + 1) * PAIRS]
    for a in range(PAIRS):
        out[:, a * LANES : (a + 1) * LANES] = buffer[pl.ds(a, count, stride=pitch_back), :].astype(bf16)


def precondition(name, pieces, tables, count, parity=None, first=0, us=1.0):
    return call(
        functools.partial(precondition_body, parity, first, len(pieces)),
        name,
        pltpu.VMEM((count, FLAT), bf16),
        [near(x) for x in (*pieces, *tables)],
        [pltpu.VMEM((max(PAIRS * (count + PAD), count * (PAIRS + PAD)), LANES), f32)],
        us=us,
    )


def scores(pieces, turned, first=0):
    x = jnp.concatenate(pieces, axis=0)
    return mm(x, turned[first : first + x.shape[1], :])


def theirs_body(store, _, turned, rest, out):
    core = position()[1]
    out[...] = turn_store(store, turned, (1 - core) * FLAT)
    rest[...] = store[:, pl.ds(pl.multiple_of(core * FLAT, FLAT), FLAT)]


def ours_body(rest, before, turned, out):
    out[...] = before[...] + turn_store(rest, turned, 0)


def woven(pieces, rows):
    first, others = pieces[0], pieces[1:-1]
    parts = [pieces[-1][...]]
    for k, other in enumerate(others):
        parts += [first[k * rows : (k + 1) * rows], other[...]]
    return parts


def scores_body(weave, turned, *refs):
    pieces = woven(refs[:-1], ROWS) if weave else [r[...] for r in refs[:-1]]
    refs[-1][...] = scores(pieces, turned)


def both_scores(name, weave, ours, far_rows, pieces, swap):
    count = sum(p.shape[0] for p in pieces)
    out = pltpu.VMEM((count, ours.shape[1]), f32)
    parts = []
    for side, turned in (("far", far_rows), ("near", ours)):
        ins = [near(x) for x in (turned, *pieces)]
        parts.append(call(functools.partial(scores_body, weave), f"{name}_{side}", out, ins, us=0.5))
    return swap(parts[0]), parts[1]


def odd_body(chips, squares, one, two, message, total):
    x = position()[0]
    total[...] = one[...] + two[...]
    count = total.shape[0] // (chips + 1)
    for block in range(chips):
        place = 1 + lax.rem(x - block + chips, chips)
        message[block * count : (block + 1) * count] = total[pl.ds(pl.multiple_of(place * count, count), count), :]
    message[chips * count :] = squares[...]


def relay_body(count, partners, squares, got, *outs):
    dim = position()[2]
    for out, partner in zip(outs, partners):
        block = partner(dim) // 2
        out[:count] = got[pl.ds(pl.multiple_of(block * count, count), count), :]
        out[count:] = squares[...] + got[got.shape[0] - squares.shape[0] :]


def send_body(chips, partners, own, one, two, *refs):
    x, _, dim = position()
    count = one.shape[0] // (chips - 1)
    for relayed, message, partner in zip(refs[: len(partners)], refs[len(partners) :], partners):
        apart = lax.rem(x - partner(dim) // 2 + chips, chips)
        there = pl.ds(pl.multiple_of(jnp.maximum(apart - 1, 0) * count, count), count)
        message[:count] = relayed[:count] + jnp.where(apart == 0, own[:count], one[there, :] + two[there, :])
        message[count:] = relayed[count:]


def finish_body(*refs):
    out, here, sem = refs[-3:]
    total = refs[0][...]
    for r in refs[1:-3]:
        total = total + r[...]
    count = out.shape[0]
    here[...] = total[:count] / jnp.sqrt(jnp.sum(total[count:], axis=0, keepdims=True) + 1e-06)
    copy = pltpu.make_async_copy(here, out, sem)
    copy.start()
    copy.wait()


def local(dims, exs, store, queries, eig_left, eig_right, val_left, val_right):
    count, rows = queries.shape[0], store.shape[0]
    chips = exs // 2
    across = [(e, e ^ 1) for e in range(exs)]

    def swap(x):
        return lax.ppermute(x, "ex", across)

    def hop(x, step):
        return lax.ppermute(x, "ex", [(e, (e + 2 * step) % exs) for e in range(exs)])

    other = swap(queries)
    tables, own = factors(queries, eig_left, eig_right, val_left, val_right)
    raw = pick(own, other)
    raw_came = [hop(raw, step) for step in range(1, chips)]
    odd_b = precondition("odd_b", (after(own, raw), other), tables, count - ROWS, 1, ROWS, us=ODDB)
    odd_b_came = [hop(odd_b, step) for step in range(1, chips)]
    turned, squares = pltpu.VMEM((FLAT, rows), bf16), pltpu.VMEM((8, rows), f32)
    outs = [turned, pltpu.VMEM((rows, FLAT), bf16), squares]
    turned_theirs, rest, part = call(theirs_body, "theirs", outs, [near(store), near(odd_b)], us=0.7)
    far_rows = swap(turned_theirs)
    ours = precondition("even", (after(own, part), other), tables, count, 0, us=EVEN)
    even_came = [hop(ours, step) for step in range(1, chips)]
    ins = [near(x) for x in (after(rest, ours), part)]
    turned_ours, squares = call(ours_body, "ours", [turned, squares], ins, us=0.6)
    odd_a = precondition("odd_a", (after(raw, squares), *raw_came), tables, chips * ROWS)

    odd_b_came = [after(x, odd_a) for x in odd_b_came]
    parts = both_scores("odd", True, turned_ours, far_rows, (odd_a, odd_b, *odd_b_came, ours), swap)
    out = pltpu.VMEM((chips * count + 8, rows), f32)
    outs = [out, pltpu.VMEM((count * (chips + 1), rows), f32)]
    message, begun = call(functools.partial(odd_body, chips), "odd", outs, [near(x) for x in (squares, *parts)], us=0.1)
    got = lax.ppermute(message, "dim", [(z, z ^ 1) for z in range(dims)])

    even_came = [after(x, message) for x in even_came]
    parts = both_scores("even", False, turned_ours, far_rows, even_came, swap)

    partners = [lambda z, k=k: lax.bitwise_xor(z, k) for k in range(0, dims, 2)]
    outs = [pltpu.VMEM((count + 8, rows), f32)] * (dims // 2)
    body = functools.partial(relay_body, count, partners)
    relayed = call(body, "relay", outs, [near(x) for x in (squares, got)], us=100.0)
    body = functools.partial(send_body, chips, partners)
    messages = call(body, "send", outs, [near(x) for x in (begun, *parts, *relayed)], us=0.2)
    sums = [messages[0]]
    for k in range(2, dims, 2):
        sums.append(lax.ppermute(messages[k // 2], "dim", [(z, z ^ k) for z in range(dims)]))
    turned = call(
        finish_body,
        "finish",
        jax.ShapeDtypeStruct((count, rows), f32),
        [near(x) for x in sums],
        [pltpu.VMEM((count, rows), f32), pltpu.SemaphoreType.DMA],
        us=0.6,
        to=HBM,
    )
    return turned.T


def solution(mesh):
    in_specs = (
        P(("grp", "ex"), "dim"),
        P(("grp", "ex"), "dim"),
        P(("grp", "dim"), None, None),
        P(("grp", "dim"), None, None),
        P(("grp", "dim"), None),
        P(("grp", "dim"), None),
    )
    out_specs = P(("grp", "ex"), "dim")
    body = functools.partial(local, mesh.shape["dim"], mesh.shape["ex"])
    return jax.shard_map(body, mesh=mesh, in_specs=in_specs, out_specs=out_specs, check_vma=False)
```

```python
import functools

import jax
import jax.numpy as jnp
from jax import lax
from jax.experimental import pallas as pl
from jax.experimental.pallas import tpu as pltpu
from jax.sharding import PartitionSpec as P

damping = 0.1
f32, bf16 = jnp.float32, jnp.bfloat16
WHOLE = pl.BlockSpec(memory_space=pltpu.VMEM)
HBM = pl.BlockSpec(memory_space=pltpu.HBM)
SIDE = 64
SCALE = 0.02
LANES = 128
PAIRS = SIDE // 2
FLAT = SIDE * SIDE
PAD = 8
EVEN = 1000.0
FACTORS = 1.2
ODDB = 1.0
PICK = 200.0
ROWS = 16


def near(x):
    return pltpu.with_memory_space_constraint(x, pltpu.VMEM)


def far(x):
    return pltpu.with_memory_space_constraint(x, pltpu.HBM)


def after(x, *others):
    return lax.optimization_barrier((x, *others))[0]


def call(body, name, outs, ins, scratch=(), us=1.0, specs=None, to=WHOLE):
    return pl.pallas_call(
        body,
        out_shape=outs,
        in_specs=specs or [WHOLE] * len(ins),
        out_specs=jax.tree.map(lambda _: to, outs, is_leaf=lambda o: hasattr(o, "shape")),
        scratch_shapes=scratch,
        cost_estimate=pl.CostEstimate(flops=int(us * 1.15e9 * SCALE), bytes_accessed=0, transcendentals=0),
        compiler_params=pltpu.CompilerParams(vmem_limit_bytes=40 * 2**20),
        name=name,
    )(*ins)


def split(x):
    high = x.astype(bf16)
    return high, (x - high.astype(f32)).astype(bf16)


def mm(a, b):
    return jnp.dot(a, b, preferred_element_type=f32)


def position():
    ex, dim = lax.axis_index("ex"), lax.axis_index("dim")
    return ex // 2, ex % 2, dim


def sides(table):
    high, low = split(table)
    return jnp.concatenate([high, high, low, low], axis=1)


def four(x):
    high, low = split(x)
    return jnp.concatenate([high, low, high, low], axis=0)


def paired(x, y):
    first = lax.broadcasted_iota(jnp.int32, x.shape, 1) < SIDE
    return jnp.where(first, x, pltpu.roll(y, SIDE, 1)), jnp.where(first, pltpu.roll(x, SIDE, 1), y)


def turn_store(store, turned, first):
    columns, rows = turned.shape
    squares = jnp.zeros((8, rows), f32)
    for column in range(0, columns, rows):
        part = store[:, pl.ds(pl.multiple_of(first + column, LANES), rows)].T
        turned[column : column + rows] = part
        part = part.astype(f32)
        squares += jnp.sum((part * part).reshape(-1, 8, rows), axis=0)
    return squares


def factors_body(*refs):
    given, refs = refs[:5], refs[5:]
    forth, back, turn, unturn, inverse, own = refs[:6]
    left, right, val_left, val_right, sems = refs[6:]
    layer = position()[1]
    copies = []
    for k, (g, h) in enumerate(zip(given, [left, right, val_left, val_right, own])):
        copies.append(pltpu.make_async_copy(g.at[layer] if k < 2 else g, h, sems.at[k]))
    for copy in copies:
        copy.start()
    for copy in copies[:4]:
        copy.wait()
    table = jnp.concatenate([left[pl.ds(low, PAIRS, stride=2), :] for low in range(2)], axis=0)
    back[...] = sides(table)
    forth[...] = sides(table.T)
    twice = jnp.concatenate([right[...]] * 2, axis=1)
    half = lax.broadcasted_iota(jnp.int32, (SIDE, LANES), 1) // SIDE
    table = jnp.concatenate([jnp.where(half == low, twice, 0.0) for low in range(2)], axis=0)
    turn[...] = jnp.concatenate(split(table), axis=0)
    both = jnp.concatenate(split(table.T), axis=1)
    unturn[...] = jnp.concatenate([both, both], axis=0)
    along = jnp.concatenate([val_right[pl.ds(layer, 1), :]] * 2, axis=1)
    down = jnp.broadcast_to(val_left[pl.ds(layer, 1), :], (SIDE, SIDE)).T
    inverse[...] = 1.0 / (jnp.concatenate([down] * 2, axis=1) * along + damping)
    copies[4].wait()


def factors(queries, left, right, val_left, val_right):
    shapes = [((64, 256), bf16)] * 2 + [((256, 128), bf16), ((256, 256), bf16), ((64, 128), f32), (queries.shape, bf16)]
    given = (left, right, val_left, val_right, queries)
    scratch = [pltpu.VMEM(x.shape[1:] if x.ndim == 3 else x.shape, f32) for x in given[:4]]
    scratch.append(pltpu.SemaphoreType.DMA((5,)))
    *tables, own = call(
        factors_body,
        "factors",
        [pltpu.VMEM(shape, kind) for shape, kind in shapes],
        [far(x) for x in given],
        scratch,
        us=FACTORS,
        specs=[HBM] * 5,
    )
    return tables, own


def pick_body(own, other, out):
    _, core, dim = position()
    part = pl.ds(pl.multiple_of(core * FLAT, FLAT), FLAT)
    out[...] = jnp.where((core + dim) % 2 == 1, own[:ROWS, part], other[:ROWS, part])


def pick(own, other):
    return call(pick_body, "pick", pltpu.VMEM((ROWS, FLAT), bf16), [near(x) for x in (own, other)], us=PICK)


def precondition_body(parity, first, pieces, *refs):
    pieces, refs = refs[:pieces], refs[pieces:]
    forth, back, turn, unturn, inverse = refs[:5]
    out, buffer = refs[5:]
    _, core, dim = position()
    count = out.shape[0]
    pitch, pitch_back = count + PAD, PAIRS + PAD
    x = []
    for a in range(PAIRS):
        if parity is None:
            x += [piece[:, a * LANES : (a + 1) * LANES] for piece in pieces]
        else:
            part = pl.ds(pl.multiple_of(core * FLAT + a * LANES, LANES), LANES)
            own, other = [piece[first : first + count, part] for piece in pieces]
            x.append(jnp.where((core + dim) % 2 == parity, own, other))
    x = jnp.concatenate(x, axis=0)
    t = mm(x, turn[:LANES]) + mm(x, turn[LANES:])
    for a in range(PAIRS):
        buffer[a * pitch : a * pitch + count] = t[a * count : (a + 1) * count]
    turned = []
    for n in range(0, count, 2):
        two = [buffer[pl.ds(n + k, PAIRS, stride=pitch), :] for k in range(2)]
        turned.append(jnp.concatenate(paired(*two), axis=0))
    t = mm(forth[...], four(jnp.concatenate(turned, axis=1)))
    t = mm(back[...], four(t * jnp.concatenate([inverse[...]] * (count // 2), axis=1)))
    rows = []
    for n in range(0, count * SIDE, LANES):
        rows += paired(t[:PAIRS, n : n + LANES], t[PAIRS:, n : n + LANES])
    t = mm(jnp.concatenate(split(jnp.concatenate(rows, axis=0)), axis=1), unturn[...])
    t = t[:, :LANES] + t[:, LANES:]
    for n in range(count):
        buffer[n * pitch_back : n * pitch_back + PAIRS] = t[n * PAIRS : (n + 1) * PAIRS]
    for a in range(PAIRS):
        out[:, a * LANES : (a + 1) * LANES] = buffer[pl.ds(a, count, stride=pitch_back), :].astype(bf16)


def precondition(name, pieces, tables, count, parity=None, first=0, us=1.0):
    return call(
        functools.partial(precondition_body, parity, first, len(pieces)),
        name,
        pltpu.VMEM((count, FLAT), bf16),
        [near(x) for x in (*pieces, *tables)],
        [pltpu.VMEM((max(PAIRS * (count + PAD), count * (PAIRS + PAD)), LANES), f32)],
        us=us,
    )


def scores(pieces, turned, first=0):
    x = jnp.concatenate(pieces, axis=0)
    return mm(x, turned[first : first + x.shape[1], :])


def theirs_body(store, _, turned, rest, out):
    core = position()[1]
    out[...] = turn_store(store, turned, (1 - core) * FLAT)
    rest[...] = store[:, pl.ds(pl.multiple_of(core * FLAT, FLAT), FLAT)]


def ours_body(rest, before, turned, out):
    out[...] = before[...] + turn_store(rest, turned, 0)


def woven(pieces, rows):
    first, others = pieces[0], pieces[1:-1]
    parts = [pieces[-1][...]]
    for k, other in enumerate(others):
        parts += [first[k * rows : (k + 1) * rows], other[...]]
    return parts


def scores_body(weave, turned, *refs):
    pieces = woven(refs[:-1], ROWS) if weave else [r[...] for r in refs[:-1]]
    refs[-1][...] = scores(pieces, turned)


def both_scores(name, weave, ours, far_rows, pieces, swap):
    count = sum(p.shape[0] for p in pieces)
    out = pltpu.VMEM((count, ours.shape[1]), f32)
    parts = []
    for side, turned in (("far", far_rows), ("near", ours)):
        ins = [near(x) for x in (turned, *pieces)]
        parts.append(call(functools.partial(scores_body, weave), f"{name}_{side}", out, ins, us=0.5))
    return swap(parts[0]), parts[1]


def odd_body(chips, squares, one, two, message, total):
    x = position()[0]
    total[...] = one[...] + two[...]
    count = total.shape[0] // (chips + 1)
    for block in range(chips):
        place = 1 + lax.rem(x - block + chips, chips)
        message[block * count : (block + 1) * count] = total[pl.ds(pl.multiple_of(place * count, count), count), :]
    message[chips * count :] = squares[...]


def relay_body(count, partners, squares, got, *outs):
    dim = position()[2]
    for out, partner in zip(outs, partners):
        block = partner(dim) // 2
        out[:count] = got[pl.ds(pl.multiple_of(block * count, count), count), :]
        out[count:] = squares[...] + got[got.shape[0] - squares.shape[0] :]


def send_body(chips, partners, own, one, two, *refs):
    x, _, dim = position()
    count = one.shape[0] // (chips - 1)
    for relayed, message, partner in zip(refs[: len(partners)], refs[len(partners) :], partners):
        apart = lax.rem(x - partner(dim) // 2 + chips, chips)
        there = pl.ds(pl.multiple_of(jnp.maximum(apart - 1, 0) * count, count), count)
        value = relayed[:count] + jnp.where(apart == 0, own[:count], one[there, :] + two[there, :])
        squares = jnp.sum(relayed[count:], axis=0, keepdims=True)
        row = lax.broadcasted_iota(jnp.int32, (8, LANES), 0)
        last = jnp.zeros((8, LANES), f32)
        for k in range(value.shape[1] // LANES):
            part = slice(k * LANES, (k + 1) * LANES)
            message[k * count : (k + 1) * count] = value[:, part]
            last = jnp.where(row == k, squares[:, part], last)
        message[message.shape[0] - 8 :] = last


def finish_body(*refs):
    out, here, sem = refs[-3:]
    total = refs[0][...]
    for r in refs[1:-3]:
        total = total + r[...]
    count, rows = out.shape
    squares = total[rows // LANES * count :]
    for k in range(rows // LANES):
        part = total[k * count : (k + 1) * count] / jnp.sqrt(squares[k : k + 1] + 1e-06)
        here[:, k * LANES : (k + 1) * LANES] = part
    copy = pltpu.make_async_copy(here, out, sem)
    copy.start()
    copy.wait()


def local(dims, exs, store, queries, eig_left, eig_right, val_left, val_right):
    count, rows = queries.shape[0], store.shape[0]
    chips = exs // 2
    across = [(e, e ^ 1) for e in range(exs)]

    def swap(x):
        return lax.ppermute(x, "ex", across)

    def hop(x, step):
        return lax.ppermute(x, "ex", [(e, (e + 2 * step) % exs) for e in range(exs)])

    other = swap(queries)
    tables, own = factors(queries, eig_left, eig_right, val_left, val_right)
    raw = pick(own, other)
    raw_came = [hop(raw, step) for step in range(1, chips)]
    odd_b = precondition("odd_b", (after(own, raw), other), tables, count - ROWS, 1, ROWS, us=ODDB)
    odd_b_came = [hop(odd_b, step) for step in range(1, chips)]
    turned, squares = pltpu.VMEM((FLAT, rows), bf16), pltpu.VMEM((8, rows), f32)
    outs = [turned, pltpu.VMEM((rows, FLAT), bf16), squares]
    turned_theirs, rest, part = call(theirs_body, "theirs", outs, [near(store), near(odd_b)], us=0.7)
    far_rows = swap(turned_theirs)
    ours = precondition("even", (after(own, part), other), tables, count, 0, us=EVEN)
    even_came = [hop(ours, step) for step in range(1, chips)]
    ins = [near(x) for x in (after(rest, ours), part)]
    turned_ours, squares = call(ours_body, "ours", [turned, squares], ins, us=0.6)
    odd_a = precondition("odd_a", (after(raw, squares), *raw_came), tables, chips * ROWS)

    odd_b_came = [after(x, odd_a) for x in odd_b_came]
    parts = both_scores("odd", True, turned_ours, far_rows, (odd_a, odd_b, *odd_b_came, ours), swap)
    out = pltpu.VMEM((chips * count + 8, rows), f32)
    outs = [out, pltpu.VMEM((count * (chips + 1), rows), f32)]
    message, begun = call(functools.partial(odd_body, chips), "odd", outs, [near(x) for x in (squares, *parts)], us=0.1)
    got = lax.ppermute(message, "dim", [(z, z ^ 1) for z in range(dims)])

    even_came = [after(x, message) for x in even_came]
    parts = both_scores("even", False, turned_ours, far_rows, even_came, swap)

    partners = [lambda z, k=k: lax.bitwise_xor(z, k) for k in range(0, dims, 2)]
    outs = [pltpu.VMEM((count + 8, rows), f32)] * (dims // 2)
    body = functools.partial(relay_body, count, partners)
    relayed = call(body, "relay", outs, [near(x) for x in (squares, got)], us=100.0)
    body = functools.partial(send_body, chips, partners)
    outs = [pltpu.VMEM((rows // LANES * count + 8, LANES), f32)] * (dims // 2)
    messages = call(body, "send", outs, [near(x) for x in (begun, *parts, *relayed)], us=0.2)
    sums = [messages[0]]
    for k in range(2, dims, 2):
        sums.append(lax.ppermute(messages[k // 2], "dim", [(z, z ^ k) for z in range(dims)]))
    turned = call(
        finish_body,
        "finish",
        jax.ShapeDtypeStruct((count, rows), f32),
        [near(x) for x in sums],
        [pltpu.VMEM((count, rows), f32), pltpu.SemaphoreType.DMA],
        us=0.6,
        to=HBM,
    )
    return turned.T


def solution(mesh):
    in_specs = (
        P(("grp", "ex"), "dim"),
        P(("grp", "ex"), "dim"),
        P(("grp", "dim"), None, None),
        P(("grp", "dim"), None, None),
        P(("grp", "dim"), None),
        P(("grp", "dim"), None),
    )
    out_specs = P(("grp", "ex"), "dim")
    body = functools.partial(local, mesh.shape["dim"], mesh.shape["ex"])
    return jax.shard_map(body, mesh=mesh, in_specs=in_specs, out_specs=out_specs, check_vma=False)
```

```python
import functools

import jax
import jax.numpy as jnp
from jax import lax
from jax.experimental import pallas as pl
from jax.experimental.pallas import tpu as pltpu
from jax.sharding import PartitionSpec as P

damping = 0.1
f32, bf16 = jnp.float32, jnp.bfloat16
WHOLE = pl.BlockSpec(memory_space=pltpu.VMEM)
HBM = pl.BlockSpec(memory_space=pltpu.HBM)
SIDE = 64
SCALE = 0.02
LANES = 128
PAIRS = SIDE // 2
FLAT = SIDE * SIDE
PAD = 8
EVEN = 1000.0
FACTORS = 1.2
ODDB = 1.0
PICK = 200.0
ROWS = 16


def near(x):
    return pltpu.with_memory_space_constraint(x, pltpu.VMEM)


def far(x):
    return pltpu.with_memory_space_constraint(x, pltpu.HBM)


def after(x, *others):
    return lax.optimization_barrier((x, *others))[0]


def call(body, name, outs, ins, scratch=(), us=1.0, specs=None, to=WHOLE):
    return pl.pallas_call(
        body,
        out_shape=outs,
        in_specs=specs or [WHOLE] * len(ins),
        out_specs=jax.tree.map(lambda _: to, outs, is_leaf=lambda o: hasattr(o, "shape")),
        scratch_shapes=scratch,
        cost_estimate=pl.CostEstimate(flops=int(us * 1.15e9 * SCALE), bytes_accessed=0, transcendentals=0),
        compiler_params=pltpu.CompilerParams(vmem_limit_bytes=40 * 2**20),
        name=name,
    )(*ins)


def split(x):
    high = x.astype(bf16)
    return high, (x - high.astype(f32)).astype(bf16)


def mm(a, b):
    return jnp.dot(a, b, preferred_element_type=f32)


def position():
    ex, dim = lax.axis_index("ex"), lax.axis_index("dim")
    return ex // 2, ex % 2, dim


def sides(table):
    high, low = split(table)
    return jnp.concatenate([high, high, low, low], axis=1)


def four(x):
    high, low = split(x)
    return jnp.concatenate([high, low, high, low], axis=0)


def paired(x, y):
    first = lax.broadcasted_iota(jnp.int32, x.shape, 1) < SIDE
    return jnp.where(first, x, pltpu.roll(y, SIDE, 1)), jnp.where(first, pltpu.roll(x, SIDE, 1), y)


def turn_store(store, turned, first):
    columns, rows = turned.shape
    squares = jnp.zeros((8, rows), f32)
    for column in range(0, columns, rows):
        part = store[:, pl.ds(pl.multiple_of(first + column, LANES), rows)].T
        turned[column : column + rows] = part
        part = part.astype(f32)
        squares += jnp.sum((part * part).reshape(-1, 8, rows), axis=0)
    return squares


def factors_body(*refs):
    given, refs = refs[:5], refs[5:]
    forth, back, turn, unturn, inverse, own = refs[:6]
    left, right, val_left, val_right, sems = refs[6:]
    layer = position()[1]
    copies = []
    for k, (g, h) in enumerate(zip(given, [left.at[:SIDE], right, val_left, val_right, own])):
        copies.append(pltpu.make_async_copy(g.at[layer] if k < 2 else g, h, sems.at[k]))
    for copy in copies:
        copy.start()
    for copy in copies[:4]:
        copy.wait()
    table = jnp.concatenate([left[pl.ds(low, PAIRS, stride=2), :] for low in range(2)], axis=0)
    back[...] = sides(table)
    forth[...] = sides(table.T)
    twice = jnp.concatenate([right[...]] * 2, axis=1)
    half = lax.broadcasted_iota(jnp.int32, (SIDE, LANES), 1) // SIDE
    table = jnp.concatenate([jnp.where(half == low, twice, 0.0) for low in range(2)], axis=0)
    turn[...] = jnp.concatenate(split(table), axis=0)
    both = jnp.concatenate(split(table.T), axis=1)
    unturn[...] = jnp.concatenate([both, both], axis=0)
    along = jnp.concatenate([val_right[pl.ds(layer, 1), :]] * 2, axis=1)
    down = jnp.broadcast_to(val_left[pl.ds(layer, 1), :], (SIDE, SIDE)).T
    inverse[...] = 1.0 / (jnp.concatenate([down] * 2, axis=1) * along + damping)
    copies[4].wait()


def factors(queries, left, right, val_left, val_right):
    shapes = [((64, 256), bf16)] * 2 + [((256, 128), bf16), ((256, 256), bf16), ((64, 128), f32), (queries.shape, bf16)]
    given = (left, right, val_left, val_right, queries)
    shapes_in = [(SIDE + PAD, SIDE), (SIDE, SIDE), val_left.shape, val_right.shape]
    scratch = [pltpu.VMEM(shape, f32) for shape in shapes_in]
    scratch.append(pltpu.SemaphoreType.DMA((5,)))
    *tables, own = call(
        factors_body,
        "factors",
        [pltpu.VMEM(shape, kind) for shape, kind in shapes],
        [far(x) for x in given],
        scratch,
        us=FACTORS,
        specs=[HBM] * 5,
    )
    return tables, own


def pick_body(own, other, out):
    _, core, dim = position()
    part = pl.ds(pl.multiple_of(core * FLAT, FLAT), FLAT)
    out[...] = jnp.where((core + dim) % 2 == 1, own[:ROWS, part], other[:ROWS, part])


def pick(own, other):
    return call(pick_body, "pick", pltpu.VMEM((ROWS, FLAT), bf16), [near(x) for x in (own, other)], us=PICK)


def precondition_body(parity, first, pieces, *refs):
    pieces, refs = refs[:pieces], refs[pieces:]
    forth, back, turn, unturn, inverse = refs[:5]
    out, buffer = refs[5:]
    _, core, dim = position()
    count = out.shape[0]
    pitch, pitch_back = count + PAD, PAIRS + PAD
    x = []
    for a in range(PAIRS):
        if parity is None:
            x += [piece[:, a * LANES : (a + 1) * LANES] for piece in pieces]
        else:
            part = pl.ds(pl.multiple_of(core * FLAT + a * LANES, LANES), LANES)
            own, other = [piece[first : first + count, part] for piece in pieces]
            x.append(jnp.where((core + dim) % 2 == parity, own, other))
    x = jnp.concatenate(x, axis=0)
    t = mm(x, turn[:LANES]) + mm(x, turn[LANES:])
    for a in range(PAIRS):
        buffer[a * pitch : a * pitch + count] = t[a * count : (a + 1) * count]
    turned = []
    for n in range(0, count, 2):
        two = [buffer[pl.ds(n + k, PAIRS, stride=pitch), :] for k in range(2)]
        turned.append(jnp.concatenate(paired(*two), axis=0))
    t = mm(forth[...], four(jnp.concatenate(turned, axis=1)))
    t = mm(back[...], four(t * jnp.concatenate([inverse[...]] * (count // 2), axis=1)))
    rows = []
    for n in range(0, count * SIDE, LANES):
        rows += paired(t[:PAIRS, n : n + LANES], t[PAIRS:, n : n + LANES])
    t = mm(jnp.concatenate(split(jnp.concatenate(rows, axis=0)), axis=1), unturn[...])
    t = t[:, :LANES] + t[:, LANES:]
    for n in range(count):
        buffer[n * pitch_back : n * pitch_back + PAIRS] = t[n * PAIRS : (n + 1) * PAIRS]
    for a in range(PAIRS):
        out[:, a * LANES : (a + 1) * LANES] = buffer[pl.ds(a, count, stride=pitch_back), :].astype(bf16)


def precondition(name, pieces, tables, count, parity=None, first=0, us=1.0):
    return call(
        functools.partial(precondition_body, parity, first, len(pieces)),
        name,
        pltpu.VMEM((count, FLAT), bf16),
        [near(x) for x in (*pieces, *tables)],
        [pltpu.VMEM((max((PAIRS + 1) * (count + PAD), (count + 1) * (PAIRS + PAD)), LANES), f32)],
        us=us,
    )


def scores(pieces, turned, first=0):
    x = jnp.concatenate(pieces, axis=0)
    return mm(x, turned[first : first + x.shape[1], :])


def theirs_body(store, _, turned, rest, out):
    core = position()[1]
    out[...] = turn_store(store, turned, (1 - core) * FLAT)
    rest[...] = store[:, pl.ds(pl.multiple_of(core * FLAT, FLAT), FLAT)]


def ours_body(rest, before, turned, out):
    out[...] = before[...] + turn_store(rest, turned, 0)


def woven(pieces, rows):
    first, others = pieces[0], pieces[1:-1]
    parts = [pieces[-1][...]]
    for k, other in enumerate(others):
        parts += [first[k * rows : (k + 1) * rows], other[...]]
    return parts


def scores_body(weave, turned, *refs):
    pieces = woven(refs[:-1], ROWS) if weave else [r[...] for r in refs[:-1]]
    refs[-1][...] = scores(pieces, turned)


def both_scores(name, weave, ours, far_rows, pieces, swap):
    count = sum(p.shape[0] for p in pieces)
    out = pltpu.VMEM((count, ours.shape[1]), f32)
    parts = []
    for side, turned in (("far", far_rows), ("near", ours)):
        ins = [near(x) for x in (turned, *pieces)]
        parts.append(call(functools.partial(scores_body, weave), f"{name}_{side}", out, ins, us=0.5))
    return swap(parts[0]), parts[1]


def odd_body(chips, squares, one, two, message, total):
    x = position()[0]
    total[...] = one[...] + two[...]
    count = total.shape[0] // (chips + 1)
    for block in range(chips):
        place = 1 + lax.rem(x - block + chips, chips)
        message[block * count : (block + 1) * count] = total[pl.ds(pl.multiple_of(place * count, count), count), :]
    message[chips * count :] = squares[...]


def relay_body(count, partners, squares, got, *outs):
    dim = position()[2]
    for out, partner in zip(outs, partners):
        block = partner(dim) // 2
        out[:count] = got[pl.ds(pl.multiple_of(block * count, count), count), :]
        out[count:] = squares[...] + got[got.shape[0] - squares.shape[0] :]


def send_body(chips, partners, own, one, two, *refs):
    x, _, dim = position()
    count = one.shape[0] // (chips - 1)
    for relayed, message, partner in zip(refs[: len(partners)], refs[len(partners) :], partners):
        apart = lax.rem(x - partner(dim) // 2 + chips, chips)
        there = pl.ds(pl.multiple_of(jnp.maximum(apart - 1, 0) * count, count), count)
        value = relayed[:count] + jnp.where(apart == 0, own[:count], one[there, :] + two[there, :])
        squares = jnp.sum(relayed[count:], axis=0, keepdims=True)
        row = lax.broadcasted_iota(jnp.int32, (8, LANES), 0)
        last = jnp.zeros((8, LANES), f32)
        for k in range(value.shape[1] // LANES):
            part = slice(k * LANES, (k + 1) * LANES)
            message[k * count : (k + 1) * count] = value[:, part]
            last = jnp.where(row == k, squares[:, part], last)
        message[message.shape[0] - 8 :] = last


def finish_body(*refs):
    out, here, sem = refs[-3:]
    total = refs[0][...]
    for r in refs[1:-3]:
        total = total + r[...]
    count, rows = out.shape
    squares = total[rows // LANES * count :]
    for k in range(rows // LANES):
        part = total[k * count : (k + 1) * count] / jnp.sqrt(squares[k : k + 1] + 1e-06)
        here[:, k * LANES : (k + 1) * LANES] = part
    copy = pltpu.make_async_copy(here, out, sem)
    copy.start()
    copy.wait()


def local(dims, exs, store, queries, eig_left, eig_right, val_left, val_right):
    count, rows = queries.shape[0], store.shape[0]
    chips = exs // 2
    across = [(e, e ^ 1) for e in range(exs)]

    def swap(x):
        return lax.ppermute(x, "ex", across)

    def hop(x, step):
        return lax.ppermute(x, "ex", [(e, (e + 2 * step) % exs) for e in range(exs)])

    other = swap(queries)
    tables, own = factors(queries, eig_left, eig_right, val_left, val_right)
    raw = pick(own, other)
    raw_came = [hop(raw, step) for step in range(1, chips)]
    odd_b = precondition("odd_b", (after(own, raw), other), tables, count - ROWS, 1, ROWS, us=ODDB)
    odd_b_came = [hop(odd_b, step) for step in range(1, chips)]
    turned, squares = pltpu.VMEM((FLAT, rows), bf16), pltpu.VMEM((8, rows), f32)
    outs = [turned, pltpu.VMEM((rows, FLAT), bf16), squares]
    turned_theirs, rest, part = call(theirs_body, "theirs", outs, [near(store), near(odd_b)], us=0.7)
    far_rows = swap(turned_theirs)
    ours = precondition("even", (after(own, part), other), tables, count, 0, us=EVEN)
    even_came = [hop(ours, step) for step in range(1, chips)]
    ins = [near(x) for x in (after(rest, ours), part)]
    turned_ours, squares = call(ours_body, "ours", [turned, squares], ins, us=0.6)
    odd_a = precondition("odd_a", (after(raw, squares), *raw_came), tables, chips * ROWS)

    odd_b_came = [after(x, odd_a) for x in odd_b_came]
    parts = both_scores("odd", True, turned_ours, far_rows, (odd_a, odd_b, *odd_b_came, ours), swap)
    out = pltpu.VMEM((chips * count + 8, rows), f32)
    outs = [out, pltpu.VMEM((count * (chips + 1), rows), f32)]
    message, begun = call(functools.partial(odd_body, chips), "odd", outs, [near(x) for x in (squares, *parts)], us=0.1)
    got = lax.ppermute(message, "dim", [(z, z ^ 1) for z in range(dims)])

    even_came = [after(x, message) for x in even_came]
    parts = both_scores("even", False, turned_ours, far_rows, even_came, swap)

    partners = [lambda z, k=k: lax.bitwise_xor(z, k) for k in range(0, dims, 2)]
    outs = [pltpu.VMEM((count + 8, rows), f32)] * (dims // 2)
    body = functools.partial(relay_body, count, partners)
    relayed = call(body, "relay", outs, [near(x) for x in (squares, got)], us=100.0)
    body = functools.partial(send_body, chips, partners)
    outs = [pltpu.VMEM((rows // LANES * count + 8, LANES), f32)] * (dims // 2)
    messages = call(body, "send", outs, [near(x) for x in (begun, *parts, *relayed)], us=0.2)
    sums = [messages[0]]
    for k in range(2, dims, 2):
        sums.append(lax.ppermute(messages[k // 2], "dim", [(z, z ^ k) for z in range(dims)]))
    turned = call(
        finish_body,
        "finish",
        jax.ShapeDtypeStruct((count, rows), f32),
        [near(x) for x in sums],
        [pltpu.VMEM((count, rows), f32), pltpu.SemaphoreType.DMA],
        us=0.6,
        to=HBM,
    )
    return turned.T


def solution(mesh):
    in_specs = (
        P(("grp", "ex"), "dim"),
        P(("grp", "ex"), "dim"),
        P(("grp", "dim"), None, None),
        P(("grp", "dim"), None, None),
        P(("grp", "dim"), None),
        P(("grp", "dim"), None),
    )
    out_specs = P(("grp", "ex"), "dim")
    body = functools.partial(local, mesh.shape["dim"], mesh.shape["ex"])
    return jax.shard_map(body, mesh=mesh, in_specs=in_specs, out_specs=out_specs, check_vma=False)
```

```python
import functools

import jax
import jax.numpy as jnp
from jax import lax
from jax.experimental import pallas as pl
from jax.experimental.pallas import tpu as pltpu
from jax.sharding import PartitionSpec as P

damping = 0.1
f32, bf16 = jnp.float32, jnp.bfloat16
WHOLE = pl.BlockSpec(memory_space=pltpu.VMEM)
HBM = pl.BlockSpec(memory_space=pltpu.HBM)
SIDE = 64
SCALE = 0.02
LANES = 128
PAIRS = SIDE // 2
FLAT = SIDE * SIDE
PAD = 8
EVEN = 1000.0
FACTORS = 1.2
ODDB = 1.0
PICK = 200.0
ROWS = 16


def near(x):
    return pltpu.with_memory_space_constraint(x, pltpu.VMEM)


def far(x):
    return pltpu.with_memory_space_constraint(x, pltpu.HBM)


def after(x, *others):
    return lax.optimization_barrier((x, *others))[0]


def call(body, name, outs, ins, scratch=(), us=1.0, specs=None, to=WHOLE):
    return pl.pallas_call(
        body,
        out_shape=outs,
        in_specs=specs or [WHOLE] * len(ins),
        out_specs=jax.tree.map(lambda _: to, outs, is_leaf=lambda o: hasattr(o, "shape")),
        scratch_shapes=scratch,
        cost_estimate=pl.CostEstimate(flops=int(us * 1.15e9 * SCALE), bytes_accessed=0, transcendentals=0),
        compiler_params=pltpu.CompilerParams(vmem_limit_bytes=40 * 2**20),
        name=name,
    )(*ins)


def split(x):
    high = x.astype(bf16)
    return high, (x - high.astype(f32)).astype(bf16)


def mm(a, b):
    return jnp.dot(a, b, preferred_element_type=f32)


def position():
    ex, dim = lax.axis_index("ex"), lax.axis_index("dim")
    return ex // 2, ex % 2, dim


def sides(table):
    high, low = split(table)
    return jnp.concatenate([high, high, low, low], axis=1)


def four(x):
    high, low = split(x)
    return jnp.concatenate([high, low, high, low], axis=0)


def paired(x, y):
    first = lax.broadcasted_iota(jnp.int32, x.shape, 1) < SIDE
    return jnp.where(first, x, pltpu.roll(y, SIDE, 1)), jnp.where(first, pltpu.roll(x, SIDE, 1), y)


def turn_store(store, turned, first):
    columns, rows = turned.shape
    squares = jnp.zeros((8, rows), f32)
    for column in range(0, columns, rows):
        part = store[:, pl.ds(pl.multiple_of(first + column, LANES), rows)].T
        turned[column : column + rows] = part
        part = part.astype(f32)
        squares += jnp.sum((part * part).reshape(-1, 8, rows), axis=0)
    return squares


def factors_body(*refs):
    given, refs = refs[:5], refs[5:]
    forth, back, turn, unturn, inverse, own = refs[:6]
    left, right, val_left, val_right, sems = refs[6:]
    layer = position()[1]
    copies = []
    for k, (g, h) in enumerate(zip(given, [left.at[:SIDE], right, val_left, val_right, own])):
        copies.append(pltpu.make_async_copy(g.at[layer] if k < 2 else g, h, sems.at[k]))
    for copy in copies:
        copy.start()
    for copy in copies[:4]:
        copy.wait()
    table = jnp.concatenate([left[pl.ds(low, PAIRS, stride=2), :] for low in range(2)], axis=0)
    back[...] = sides(table)
    forth[...] = sides(table.T)
    twice = jnp.concatenate([right[...]] * 2, axis=1)
    half = lax.broadcasted_iota(jnp.int32, (SIDE, LANES), 1) // SIDE
    table = jnp.concatenate([jnp.where(half == low, twice, 0.0) for low in range(2)], axis=0)
    turn[...] = jnp.concatenate(split(table), axis=0)
    both = jnp.concatenate(split(table.T), axis=1)
    unturn[...] = jnp.concatenate([both, both], axis=0)
    along = jnp.concatenate([val_right[pl.ds(layer, 1), :]] * 2, axis=1)
    down = jnp.broadcast_to(val_left[pl.ds(layer, 1), :], (SIDE, SIDE)).T
    inverse[...] = 1.0 / (jnp.concatenate([down] * 2, axis=1) * along + damping)
    copies[4].wait()


def factors(queries, left, right, val_left, val_right):
    shapes = [((64, 256), bf16)] * 2 + [((256, 128), bf16), ((256, 256), bf16), ((64, 128), f32), (queries.shape, bf16)]
    given = (left, right, val_left, val_right, queries)
    shapes_in = [(SIDE + PAD, SIDE), (SIDE, SIDE), val_left.shape, val_right.shape]
    scratch = [pltpu.VMEM(shape, f32) for shape in shapes_in]
    scratch.append(pltpu.SemaphoreType.DMA((5,)))
    *tables, own = call(
        factors_body,
        "factors",
        [pltpu.VMEM(shape, kind) for shape, kind in shapes],
        [far(x) for x in given],
        scratch,
        us=FACTORS,
        specs=[HBM] * 5,
    )
    return tables, own


def pick_body(own, other, out):
    _, core, dim = position()
    part = pl.ds(pl.multiple_of(core * FLAT, FLAT), FLAT)
    out[...] = jnp.where((core + dim) % 2 == 1, own[:ROWS, part], other[:ROWS, part])


def pick(own, other):
    return call(pick_body, "pick", pltpu.VMEM((ROWS, FLAT), bf16), [near(x) for x in (own, other)], us=PICK)


def precondition_body(parity, first, pieces, *refs):
    pieces, refs = refs[:pieces], refs[pieces:]
    forth, back, turn, unturn, inverse = refs[:5]
    out, buffer = refs[5:]
    _, core, dim = position()
    count = out.shape[0]
    pitch, pitch_back = count + PAD, PAIRS + PAD
    x = []
    for a in range(PAIRS):
        if parity is None:
            x += [piece[:, a * LANES : (a + 1) * LANES] for piece in pieces]
        else:
            part = pl.ds(pl.multiple_of(core * FLAT + a * LANES, LANES), LANES)
            own, other = [piece[first : first + count, part] for piece in pieces]
            x.append(jnp.where((core + dim) % 2 == parity, own, other))
    x = jnp.concatenate(x, axis=0)
    t = mm(x, turn[:LANES]) + mm(x, turn[LANES:])
    for a in range(PAIRS):
        buffer[a * pitch : a * pitch + count] = t[a * count : (a + 1) * count]
    turned = []
    for n in range(0, count, 2):
        two = [buffer[pl.ds(n + k, PAIRS, stride=pitch), :] for k in range(2)]
        turned.append(jnp.concatenate(paired(*two), axis=0))
    t = mm(forth[...], four(jnp.concatenate(turned, axis=1)))
    t = mm(back[...], four(t * jnp.concatenate([inverse[...]] * (count // 2), axis=1)))
    rows = []
    for n in range(0, count * SIDE, LANES):
        rows += paired(t[:PAIRS, n : n + LANES], t[PAIRS:, n : n + LANES])
    t = mm(jnp.concatenate(split(jnp.concatenate(rows, axis=0)), axis=1), unturn[...])
    t = t[:, :LANES] + t[:, LANES:]
    for n in range(count):
        buffer[n * pitch_back : n * pitch_back + PAIRS] = t[n * PAIRS : (n + 1) * PAIRS]
    for a in range(PAIRS):
        out[:, a * LANES : (a + 1) * LANES] = buffer[pl.ds(a, count, stride=pitch_back), :].astype(bf16)


def precondition(name, pieces, tables, count, parity=None, first=0, us=1.0):
    return call(
        functools.partial(precondition_body, parity, first, len(pieces)),
        name,
        pltpu.VMEM((count, FLAT), bf16),
        [near(x) for x in (*pieces, *tables)],
        [pltpu.VMEM((max((PAIRS + 1) * (count + PAD), (count + 1) * (PAIRS + PAD)), LANES), f32)],
        us=us,
    )


def scores(pieces, turned, first=0):
    x = jnp.concatenate(pieces, axis=0)
    return mm(x, turned[first : first + x.shape[1], :])


def theirs_body(store, _, turned, out):
    out[...] = turn_store(store, turned, (1 - position()[1]) * FLAT)


def ours_body(store, before, turned, out):
    out[...] = before[...] + turn_store(store, turned, position()[1] * FLAT)


def woven(pieces, rows):
    first, others = pieces[0], pieces[1:-1]
    parts = [pieces[-1][...]]
    for k, other in enumerate(others):
        parts += [first[k * rows : (k + 1) * rows], other[...]]
    return parts


def scores_body(weave, turned, *refs):
    pieces = woven(refs[:-1], ROWS) if weave else [r[...] for r in refs[:-1]]
    refs[-1][...] = scores(pieces, turned)


def both_scores(name, weave, ours, far_rows, pieces, swap):
    count = sum(p.shape[0] for p in pieces)
    out = pltpu.VMEM((count, ours.shape[1]), f32)
    parts = []
    for side, turned in (("far", far_rows), ("near", ours)):
        ins = [near(x) for x in (turned, *pieces)]
        parts.append(call(functools.partial(scores_body, weave), f"{name}_{side}", out, ins, us=0.5))
    return swap(parts[0]), parts[1]


def odd_body(chips, squares, one, two, message, total):
    x = position()[0]
    total[...] = one[...] + two[...]
    count = total.shape[0] // (chips + 1)
    for block in range(chips):
        place = 1 + lax.rem(x - block + chips, chips)
        message[block * count : (block + 1) * count] = total[pl.ds(pl.multiple_of(place * count, count), count), :]
    message[chips * count :] = squares[...]


def relay_body(count, partners, squares, got, *outs):
    dim = position()[2]
    for out, partner in zip(outs, partners):
        block = partner(dim) // 2
        out[:count] = got[pl.ds(pl.multiple_of(block * count, count), count), :]
        out[count:] = squares[...] + got[got.shape[0] - squares.shape[0] :]


def send_body(chips, partners, own, one, two, *refs):
    x, _, dim = position()
    count = one.shape[0] // (chips - 1)
    for relayed, message, partner in zip(refs[: len(partners)], refs[len(partners) :], partners):
        apart = lax.rem(x - partner(dim) // 2 + chips, chips)
        there = pl.ds(pl.multiple_of(jnp.maximum(apart - 1, 0) * count, count), count)
        value = relayed[:count] + jnp.where(apart == 0, own[:count], one[there, :] + two[there, :])
        squares = jnp.sum(relayed[count:], axis=0, keepdims=True)
        row = lax.broadcasted_iota(jnp.int32, (8, LANES), 0)
        last = jnp.zeros((8, LANES), f32)
        for k in range(value.shape[1] // LANES):
            part = slice(k * LANES, (k + 1) * LANES)
            message[k * count : (k + 1) * count] = value[:, part]
            last = jnp.where(row == k, squares[:, part], last)
        message[message.shape[0] - 8 :] = last


def finish_body(*refs):
    out, here, sem = refs[-3:]
    total = refs[0][...]
    for r in refs[1:-3]:
        total = total + r[...]
    count, rows = out.shape
    squares = total[rows // LANES * count :]
    for k in range(rows // LANES):
        part = total[k * count : (k + 1) * count] / jnp.sqrt(squares[k : k + 1] + 1e-06)
        here[:, k * LANES : (k + 1) * LANES] = part
    copy = pltpu.make_async_copy(here, out, sem)
    copy.start()
    copy.wait()


def local(dims, exs, store, queries, eig_left, eig_right, val_left, val_right):
    count, rows = queries.shape[0], store.shape[0]
    chips = exs // 2
    across = [(e, e ^ 1) for e in range(exs)]

    def swap(x):
        return lax.ppermute(x, "ex", across)

    def hop(x, step):
        return lax.ppermute(x, "ex", [(e, (e + 2 * step) % exs) for e in range(exs)])

    other = swap(queries)
    tables, own = factors(queries, eig_left, eig_right, val_left, val_right)
    raw = pick(own, other)
    raw_came = [hop(raw, step) for step in range(1, chips)]
    odd_b = precondition("odd_b", (after(own, raw), other), tables, count - ROWS, 1, ROWS, us=ODDB)
    odd_b_came = [hop(odd_b, step) for step in range(1, chips)]
    turned, squares = pltpu.VMEM((FLAT, rows), bf16), pltpu.VMEM((8, rows), f32)
    turned_theirs, part = call(theirs_body, "theirs", [turned, squares], [near(store), near(odd_b)], us=0.7)
    far_rows = swap(turned_theirs)
    ours = precondition("even", (after(own, part), other), tables, count, 0, us=EVEN)
    even_came = [hop(ours, step) for step in range(1, chips)]
    ins = [near(x) for x in (after(store, ours), part)]
    turned_ours, squares = call(ours_body, "ours", [turned, squares], ins, us=0.6)
    odd_a = precondition("odd_a", (after(raw, squares), *raw_came), tables, chips * ROWS)

    odd_b_came = [after(x, odd_a) for x in odd_b_came]
    parts = both_scores("odd", True, turned_ours, far_rows, (odd_a, odd_b, *odd_b_came, ours), swap)
    out = pltpu.VMEM((chips * count + 8, rows), f32)
    outs = [out, pltpu.VMEM((count * (chips + 1), rows), f32)]
    message, begun = call(functools.partial(odd_body, chips), "odd", outs, [near(x) for x in (squares, *parts)], us=0.1)
    got = lax.ppermute(message, "dim", [(z, z ^ 1) for z in range(dims)])

    even_came = [after(x, message) for x in even_came]
    parts = both_scores("even", False, turned_ours, far_rows, even_came, swap)

    partners = [lambda z, k=k: lax.bitwise_xor(z, k) for k in range(0, dims, 2)]
    outs = [pltpu.VMEM((count + 8, rows), f32)] * (dims // 2)
    body = functools.partial(relay_body, count, partners)
    relayed = call(body, "relay", outs, [near(x) for x in (squares, got)], us=100.0)
    body = functools.partial(send_body, chips, partners)
    outs = [pltpu.VMEM((rows // LANES * count + 8, LANES), f32)] * (dims // 2)
    messages = call(body, "send", outs, [near(x) for x in (begun, *parts, *relayed)], us=0.2)
    sums = [messages[0]]
    for k in range(2, dims, 2):
        sums.append(lax.ppermute(messages[k // 2], "dim", [(z, z ^ k) for z in range(dims)]))
    turned = call(
        finish_body,
        "finish",
        jax.ShapeDtypeStruct((count, rows), f32),
        [near(x) for x in sums],
        [pltpu.VMEM((count, rows), f32), pltpu.SemaphoreType.DMA],
        us=0.6,
        to=HBM,
    )
    return turned.T


def solution(mesh):
    in_specs = (
        P(("grp", "ex"), "dim"),
        P(("grp", "ex"), "dim"),
        P(("grp", "dim"), None, None),
        P(("grp", "dim"), None, None),
        P(("grp", "dim"), None),
        P(("grp", "dim"), None),
    )
    out_specs = P(("grp", "ex"), "dim")
    body = functools.partial(local, mesh.shape["dim"], mesh.shape["ex"])
    return jax.shard_map(body, mesh=mesh, in_specs=in_specs, out_specs=out_specs, check_vma=False)
```

```python
import functools

import jax
import jax.numpy as jnp
from jax import lax
from jax.experimental import pallas as pl
from jax.experimental.pallas import tpu as pltpu
from jax.sharding import PartitionSpec as P

damping = 0.1
f32, bf16 = jnp.float32, jnp.bfloat16
WHOLE = pl.BlockSpec(memory_space=pltpu.VMEM)
HBM = pl.BlockSpec(memory_space=pltpu.HBM)
SIDE = 64
SCALE = 0.02
LANES = 128
PAIRS = SIDE // 2
FLAT = SIDE * SIDE
PAD = 8
EVEN = 1000.0
FACTORS = 1.2
ODDB = 1.0
PICK = 200.0
ROWS = 16


def near(x):
    return pltpu.with_memory_space_constraint(x, pltpu.VMEM)


def far(x):
    return pltpu.with_memory_space_constraint(x, pltpu.HBM)


def after(x, *others):
    return lax.optimization_barrier((x, *others))[0]


def call(body, name, outs, ins, scratch=(), us=1.0, specs=None, to=WHOLE, aliases=()):
    return pl.pallas_call(
        body,
        out_shape=outs,
        in_specs=specs or [WHOLE] * len(ins),
        out_specs=jax.tree.map(lambda _: to, outs, is_leaf=lambda o: hasattr(o, "shape")),
        scratch_shapes=scratch,
        input_output_aliases=dict(aliases),
        cost_estimate=pl.CostEstimate(flops=int(us * 1.15e9 * SCALE), bytes_accessed=0, transcendentals=0),
        compiler_params=pltpu.CompilerParams(vmem_limit_bytes=40 * 2**20),
        name=name,
    )(*ins)


def split(x):
    high = x.astype(bf16)
    return high, (x - high.astype(f32)).astype(bf16)


def mm(a, b):
    return jnp.dot(a, b, preferred_element_type=f32)


def position():
    ex, dim = lax.axis_index("ex"), lax.axis_index("dim")
    return ex // 2, ex % 2, dim


def sides(table):
    high, low = split(table)
    return jnp.concatenate([high, high, low, low], axis=1)


def four(x):
    high, low = split(x)
    return jnp.concatenate([high, low, high, low], axis=0)


def paired(x, y):
    first = lax.broadcasted_iota(jnp.int32, x.shape, 1) < SIDE
    return jnp.where(first, x, pltpu.roll(y, SIDE, 1)), jnp.where(first, pltpu.roll(x, SIDE, 1), y)


def turn_store(store, turned, first):
    columns, rows = turned.shape
    squares = jnp.zeros((8, rows), f32)
    for column in range(0, columns, rows):
        part = store[:, pl.ds(pl.multiple_of(first + column, LANES), rows)].T
        turned[column : column + rows] = part
        part = part.astype(f32)
        squares += jnp.sum((part * part).reshape(-1, 8, rows), axis=0)
    return squares


def factors_body(*refs):
    given, refs = refs[:5], refs[5:]
    forth, back, turn, unturn, inverse, own = refs[:6]
    left, right, val_left, val_right, sems = refs[6:]
    layer = position()[1]
    copies = []
    for k, (g, h) in enumerate(zip(given, [left.at[:SIDE], right, val_left, val_right, own])):
        copies.append(pltpu.make_async_copy(g.at[layer] if k < 2 else g, h, sems.at[k]))
    for copy in copies:
        copy.start()
    for copy in copies[:4]:
        copy.wait()
    table = jnp.concatenate([left[pl.ds(low, PAIRS, stride=2), :] for low in range(2)], axis=0)
    back[...] = sides(table)
    forth[...] = sides(table.T)
    twice = jnp.concatenate([right[...]] * 2, axis=1)
    half = lax.broadcasted_iota(jnp.int32, (SIDE, LANES), 1) // SIDE
    table = jnp.concatenate([jnp.where(half == low, twice, 0.0) for low in range(2)], axis=0)
    turn[...] = jnp.concatenate(split(table), axis=0)
    both = jnp.concatenate(split(table.T), axis=1)
    unturn[...] = jnp.concatenate([both, both], axis=0)
    along = jnp.concatenate([val_right[pl.ds(layer, 1), :]] * 2, axis=1)
    down = jnp.broadcast_to(val_left[pl.ds(layer, 1), :], (SIDE, SIDE)).T
    inverse[...] = 1.0 / (jnp.concatenate([down] * 2, axis=1) * along + damping)
    copies[4].wait()


def factors(queries, left, right, val_left, val_right):
    shapes = [((64, 256), bf16)] * 2 + [((256, 128), bf16), ((256, 256), bf16), ((64, 128), f32), (queries.shape, bf16)]
    given = (left, right, val_left, val_right, queries)
    shapes_in = [(SIDE + PAD, SIDE), (SIDE, SIDE), val_left.shape, val_right.shape]
    scratch = [pltpu.VMEM(shape, f32) for shape in shapes_in]
    scratch.append(pltpu.SemaphoreType.DMA((5,)))
    *tables, own = call(
        factors_body,
        "factors",
        [pltpu.VMEM(shape, kind) for shape, kind in shapes],
        [far(x) for x in given],
        scratch,
        us=FACTORS,
        specs=[HBM] * 5,
    )
    return tables, own


def pick_body(own, other, out):
    _, core, dim = position()
    part = pl.ds(pl.multiple_of(core * FLAT, FLAT), FLAT)
    out[...] = jnp.where((core + dim) % 2 == 1, own[:ROWS, part], other[:ROWS, part])


def pick(own, other):
    return call(pick_body, "pick", pltpu.VMEM((ROWS, FLAT), bf16), [near(x) for x in (own, other)], us=PICK)


def precondition_body(parity, first, pieces, *refs):
    pieces, refs = refs[:pieces], refs[pieces:]
    forth, back, turn, unturn, inverse = refs[:5]
    out, buffer = refs[5:]
    _, core, dim = position()
    count = out.shape[0]
    pitch, pitch_back = count + PAD, PAIRS + PAD
    x = []
    for a in range(PAIRS):
        if parity is None:
            x += [piece[:, a * LANES : (a + 1) * LANES] for piece in pieces]
        else:
            part = pl.ds(pl.multiple_of(core * FLAT + a * LANES, LANES), LANES)
            own, other = [piece[first : first + count, part] for piece in pieces]
            x.append(jnp.where((core + dim) % 2 == parity, own, other))
    x = jnp.concatenate(x, axis=0)
    t = mm(x, turn[:LANES]) + mm(x, turn[LANES:])
    for a in range(PAIRS):
        buffer[a * pitch : a * pitch + count] = t[a * count : (a + 1) * count]
    turned = []
    for n in range(0, count, 2):
        two = [buffer[pl.ds(n + k, PAIRS, stride=pitch), :] for k in range(2)]
        turned.append(jnp.concatenate(paired(*two), axis=0))
    t = mm(forth[...], four(jnp.concatenate(turned, axis=1)))
    t = mm(back[...], four(t * jnp.concatenate([inverse[...]] * (count // 2), axis=1)))
    rows = []
    for n in range(0, count * SIDE, LANES):
        rows += paired(t[:PAIRS, n : n + LANES], t[PAIRS:, n : n + LANES])
    t = mm(jnp.concatenate(split(jnp.concatenate(rows, axis=0)), axis=1), unturn[...])
    t = t[:, :LANES] + t[:, LANES:]
    for n in range(count):
        buffer[n * pitch_back : n * pitch_back + PAIRS] = t[n * PAIRS : (n + 1) * PAIRS]
    for a in range(PAIRS):
        out[:, a * LANES : (a + 1) * LANES] = buffer[pl.ds(a, count, stride=pitch_back), :].astype(bf16)


def precondition(name, pieces, tables, count, parity=None, first=0, us=1.0):
    return call(
        functools.partial(precondition_body, parity, first, len(pieces)),
        name,
        pltpu.VMEM((count, FLAT), bf16),
        [near(x) for x in (*pieces, *tables)],
        [pltpu.VMEM((max((PAIRS + 1) * (count + PAD), (count + 1) * (PAIRS + PAD)), LANES), f32)],
        us=us,
    )


def scores(pieces, turned, first=0):
    x = jnp.concatenate(pieces, axis=0)
    return mm(x, turned[first : first + x.shape[1], :])


def theirs_body(store, _, turned, ours, out):
    core = position()[1]
    out[...] = turn_store(store, turned, (1 - core) * FLAT)

    @pl.when(core == 1)
    def _():
        out[...] += turn_store(store, ours, FLAT)


def ours_body(store, before, _, turned, out):
    out[...] = before[...]

    @pl.when(position()[1] == 0)
    def _():
        out[...] += turn_store(store, turned, 0)


def woven(pieces, rows):
    first, others = pieces[0], pieces[1:-1]
    parts = [pieces[-1][...]]
    for k, other in enumerate(others):
        parts += [first[k * rows : (k + 1) * rows], other[...]]
    return parts


def scores_body(weave, turned, *refs):
    pieces = woven(refs[:-1], ROWS) if weave else [r[...] for r in refs[:-1]]
    refs[-1][...] = scores(pieces, turned)


def both_scores(name, weave, ours, far_rows, pieces, swap):
    count = sum(p.shape[0] for p in pieces)
    out = pltpu.VMEM((count, ours.shape[1]), f32)
    parts = []
    for side, turned in (("far", far_rows), ("near", ours)):
        ins = [near(x) for x in (turned, *pieces)]
        parts.append(call(functools.partial(scores_body, weave), f"{name}_{side}", out, ins, us=0.5))
    return swap(parts[0]), parts[1]


def odd_body(chips, squares, one, two, message, total):
    x = position()[0]
    total[...] = one[...] + two[...]
    count = total.shape[0] // (chips + 1)
    for block in range(chips):
        place = 1 + lax.rem(x - block + chips, chips)
        message[block * count : (block + 1) * count] = total[pl.ds(pl.multiple_of(place * count, count), count), :]
    message[chips * count :] = squares[...]


def relay_body(count, partners, squares, got, *outs):
    dim = position()[2]
    for out, partner in zip(outs, partners):
        block = partner(dim) // 2
        out[:count] = got[pl.ds(pl.multiple_of(block * count, count), count), :]
        out[count:] = squares[...] + got[got.shape[0] - squares.shape[0] :]


def send_body(chips, partners, own, one, two, *refs):
    x, _, dim = position()
    count = one.shape[0] // (chips - 1)
    for relayed, message, partner in zip(refs[: len(partners)], refs[len(partners) :], partners):
        apart = lax.rem(x - partner(dim) // 2 + chips, chips)
        there = pl.ds(pl.multiple_of(jnp.maximum(apart - 1, 0) * count, count), count)
        value = relayed[:count] + jnp.where(apart == 0, own[:count], one[there, :] + two[there, :])
        squares = jnp.sum(relayed[count:], axis=0, keepdims=True)
        row = lax.broadcasted_iota(jnp.int32, (8, LANES), 0)
        last = jnp.zeros((8, LANES), f32)
        for k in range(value.shape[1] // LANES):
            part = slice(k * LANES, (k + 1) * LANES)
            message[k * count : (k + 1) * count] = value[:, part]
            last = jnp.where(row == k, squares[:, part], last)
        message[message.shape[0] - 8 :] = last


def finish_body(*refs):
    out, here, sem = refs[-3:]
    total = refs[0][...]
    for r in refs[1:-3]:
        total = total + r[...]
    count, rows = out.shape
    squares = total[rows // LANES * count :]
    for k in range(rows // LANES):
        part = total[k * count : (k + 1) * count] / jnp.sqrt(squares[k : k + 1] + 1e-06)
        here[:, k * LANES : (k + 1) * LANES] = part
    copy = pltpu.make_async_copy(here, out, sem)
    copy.start()
    copy.wait()


def local(dims, exs, store, queries, eig_left, eig_right, val_left, val_right):
    count, rows = queries.shape[0], store.shape[0]
    chips = exs // 2
    across = [(e, e ^ 1) for e in range(exs)]

    def swap(x):
        return lax.ppermute(x, "ex", across)

    def hop(x, step):
        return lax.ppermute(x, "ex", [(e, (e + 2 * step) % exs) for e in range(exs)])

    other = swap(queries)
    tables, own = factors(queries, eig_left, eig_right, val_left, val_right)
    raw = pick(own, other)
    raw_came = [hop(raw, step) for step in range(1, chips)]
    odd_b = precondition("odd_b", (after(own, raw), other), tables, count - ROWS, 1, ROWS, us=ODDB)
    odd_b_came = [hop(odd_b, step) for step in range(1, chips)]
    turned, squares = pltpu.VMEM((FLAT, rows), bf16), pltpu.VMEM((8, rows), f32)
    turned_theirs, turned_ours, part = call(theirs_body, "theirs", [turned, turned, squares], [near(store), near(odd_b)], us=0.7)
    far_rows = swap(turned_theirs)
    ours = precondition("even", (after(own, part), other), tables, count, 0, us=EVEN)
    even_came = [hop(ours, step) for step in range(1, chips)]
    ins = [near(x) for x in (after(store, ours), part, turned_ours)]
    turned_ours, squares = call(ours_body, "ours", [turned, squares], ins, us=0.6, aliases=[(2, 0)])
    odd_a = precondition("odd_a", (after(raw, squares), *raw_came), tables, chips * ROWS)

    odd_b_came = [after(x, odd_a) for x in odd_b_came]
    parts = both_scores("odd", True, turned_ours, far_rows, (odd_a, odd_b, *odd_b_came, ours), swap)
    out = pltpu.VMEM((chips * count + 8, rows), f32)
    outs = [out, pltpu.VMEM((count * (chips + 1), rows), f32)]
    message, begun = call(functools.partial(odd_body, chips), "odd", outs, [near(x) for x in (squares, *parts)], us=0.1)
    got = lax.ppermute(message, "dim", [(z, z ^ 1) for z in range(dims)])

    even_came = [after(x, message) for x in even_came]
    parts = both_scores("even", False, turned_ours, far_rows, even_came, swap)

    partners = [lambda z, k=k: lax.bitwise_xor(z, k) for k in range(0, dims, 2)]
    outs = [pltpu.VMEM((count + 8, rows), f32)] * (dims // 2)
    body = functools.partial(relay_body, count, partners)
    relayed = call(body, "relay", outs, [near(x) for x in (squares, got)], us=100.0)
    body = functools.partial(send_body, chips, partners)
    outs = [pltpu.VMEM((rows // LANES * count + 8, LANES), f32)] * (dims // 2)
    messages = call(body, "send", outs, [near(x) for x in (begun, *parts, *relayed)], us=0.2)
    sums = [messages[0]]
    for k in range(2, dims, 2):
        sums.append(lax.ppermute(messages[k // 2], "dim", [(z, z ^ k) for z in range(dims)]))
    turned = call(
        finish_body,
        "finish",
        jax.ShapeDtypeStruct((count, rows), f32),
        [near(x) for x in sums],
        [pltpu.VMEM((count, rows), f32), pltpu.SemaphoreType.DMA],
        us=0.6,
        to=HBM,
    )
    return turned.T


def solution(mesh):
    in_specs = (
        P(("grp", "ex"), "dim"),
        P(("grp", "ex"), "dim"),
        P(("grp", "dim"), None, None),
        P(("grp", "dim"), None, None),
        P(("grp", "dim"), None),
        P(("grp", "dim"), None),
    )
    out_specs = P(("grp", "ex"), "dim")
    body = functools.partial(local, mesh.shape["dim"], mesh.shape["ex"])
    return jax.shard_map(body, mesh=mesh, in_specs=in_specs, out_specs=out_specs, check_vma=False)
```
